256 devices in a mesh: seg: 8 (over y, core), op: 32 (over x, z).
Axes of the slice: x: 4, y: 4, z: 8, core: 2. Of those that a mesh axis runs over, the one named last changes fastest.
Arguments:
- left_ops: float32 [8, 32, 768, 768], P('seg', 'op'), as said below
- right_ops: float32 [8, 32, 768, 768], P('seg', 'op'), as said below
- wavefunction: float32 [8, 768, 768], P('seg', 'op'), as said below
- basis_rotation: float32 [8, 768, 768], P('seg'), may hold values from -0.21875 to 0.21875
- pair_term: int32 [8, 32], P('seg', 'op'), may hold values from 0 to 15
- coupling: float32 [16], replicated, may hold values from 0.1 to 1
- left_charge: int32 [8, 768], P('seg'), may hold values from 0 to 2, as said below
- right_charge: int32 [8, 768], P('seg'), may hold values from 0 to 2, as said below
Outputs:
- chebyshev: float32 [8, 768, 768], P('seg', 'op')
- energy: float32 [8], P('seg')
- handed: float32 [8, 32, 768, 768], P('seg', 'op')
The draws below stay inside these ranges and needn't reach their ends.
Inputs may be any that keep to these rules, and one draw needn't show every extreme that they name: `left_ops`: each operator is a dominant positive diagonal plus dense full-rank off-diagonal entries. `right_ops`: each operator is a dominant positive diagonal plus dense full-rank off-diagonal entries. `wavefunction`: dense real entries of varying scale. `left_charge`: in each segment exactly 256 left bond states carry each quantum number. `right_charge`: in each segment exactly 256 right bond states carry each quantum number.
All inputs are finite; a program needn't handle non-finite values.
Results may differ from the reference program's by a relative error of at most 0.0003.
Values sent between devices are 32-bit elements; how exact they have to be, the bound alone decides.
A program may use at most 128 MiB of HBM per device.

```python
import math
import jax
import jax.numpy as jnp
from jax import lax

M = 768
NTERMS = 16
NQ = 3
PAIRS = 32
SEGS = 8


def operator_stack(key):
    first_key, second_key = jax.random.split(key)
    scatter_part = jax.random.normal(first_key, (SEGS, PAIRS, M, M), jnp.float32) * M ** (-0.5)
    diagonal = jnp.exp(jax.random.uniform(second_key, (SEGS, PAIRS, 1, M), jnp.float32, 0.0, math.log(2.0)))
    identity = jnp.eye(M, dtype=jnp.float32)
    return scatter_part + identity * diagonal


def draw_left_ops(key, part):
    return operator_stack(jax.random.fold_in(key, 101))


def draw_right_ops(key, part):
    return operator_stack(jax.random.fold_in(key, 202))


def draw_wavefunction(key, part):
    base_key = jax.random.fold_in(key, 303)
    first_key, second_key, third_key = jax.random.split(base_key, 3)
    values = jax.random.normal(first_key, (SEGS, M, M), jnp.float32)
    rising = 3.0 ** (jnp.arange(M, dtype=jnp.float32) / M)
    row_scale = jnp.exp(jax.random.uniform(second_key, (SEGS, M, 1), jnp.float32, 0.0, math.log(10.0))) * rising[None, :, None]
    column_scale = jnp.exp(jax.random.uniform(third_key, (SEGS, 1, M), jnp.float32, 0.0, math.log(10.0)))
    return values * row_scale * column_scale


def balanced_charges(key):
    pattern = jnp.arange(M, dtype=jnp.int32) % NQ
    keys = jax.random.split(key, SEGS)
    return jax.vmap(lambda k: jax.random.permutation(k, pattern))(keys).astype(jnp.int32)


def draw_left_charge(key, part):
    return balanced_charges(jax.random.fold_in(key, 404))


def draw_right_charge(key, part):
    return balanced_charges(jax.random.fold_in(key, 505))


def touch_ends(result, stream_key, low, high):
    place = [jax.random.randint(jax.random.fold_in(stream_key, axis), (), 0, length) for axis, length in enumerate(result.shape)]
    main_axis = result.shape.index(max(result.shape))
    neighbour = place[:main_axis] + [(place[main_axis] + 1) % result.shape[main_axis]] + place[main_axis + 1:]
    return result.at[tuple(place)].set(low).at[tuple(neighbour)].set(high)


def block_scale(own_key, extent, cuts, least, largest):
    def one(position, shards_of):
        steps = jax.random.uniform(jax.random.fold_in(jax.random.fold_in(own_key, 6), position), (shards_of,), jnp.float32, least / len(cuts), largest / len(cuts))
        return jnp.repeat(jnp.exp(steps), extent[position] // shards_of).reshape((-1,) + (1,) * (len(extent) - position - 1))

    gain = one(*cuts[0])
    for cut in cuts[1:]:
        gain = gain * one(*cut)
    return gain


def bell_draw(key, extent, deviation, reach, shards=(), kind=jnp.bfloat16):
    entries = deviation * jax.random.normal(key, extent, jnp.float32)
    if shards:
        entries = entries * block_scale(key, extent, shards, -0.22, 0.18)
    return jnp.clip(entries, -reach, reach).astype(kind)


def setup_inputs(seed: int = 0) -> dict:
    splits = jax.random.split(jax.random.key(seed), 9)
    left_ops = draw_left_ops(jax.random.fold_in(splits[8], 71), 0)
    right_ops = draw_right_ops(jax.random.fold_in(splits[8], 71), 0)
    wavefunction = draw_wavefunction(jax.random.fold_in(splits[8], 71), 0)
    basis_rotation = bell_draw(splits[3], (SEGS, M, M), M ** -0.5, 0.21875, ((0, 8),), jnp.float32)
    pair_term = touch_ends(jax.random.randint(splits[4], (SEGS, PAIRS), 0, NTERMS), jax.random.fold_in(splits[4], 1), 0, NTERMS - 1).astype(jnp.int32)
    coupling = jnp.clip(jnp.exp(jax.random.uniform(splits[5], (NTERMS,), jnp.float32, math.log(0.1), math.log(1.0))), 0.1, 1.0)
    left_charge = draw_left_charge(jax.random.fold_in(splits[8], 71), 0)
    right_charge = draw_right_charge(jax.random.fold_in(splits[8], 71), 0)
    return {"left_ops": left_ops, "right_ops": right_ops, "wavefunction": wavefunction, "basis_rotation": basis_rotation, "pair_term": pair_term, "coupling": coupling, "left_charge": left_charge, "right_charge": right_charge}


HIGH = lax.Precision.HIGHEST

def apply_operator(vector, left_ops, right_ops, coefficient, sector_mask):
    partial_value = jnp.einsum('kab,bc->kac', left_ops, vector, precision=HIGH)
    partial_value = partial_value * coefficient[:, None, None]
    total = jnp.einsum('kac,kcd->ad', partial_value, right_ops, precision=HIGH)
    return total * sector_mask

def one_segment(items):
    left_ops, right_ops, wavefunction, basis_rotation, pair_term, coupling, left_charge, right_charge = items
    sector_mask = (left_charge[:, None] == right_charge[None, :]).astype(jnp.float32)
    coefficient = coupling[pair_term]
    width = float(M * M)
    masked = sector_mask * wavefunction
    initial = masked / jnp.sqrt(jnp.sum(masked * masked) / width + 1e-06)
    image_one = apply_operator(initial, left_ops, right_ops, coefficient, sector_mask)
    energy = jnp.sum(initial * image_one) / width
    spread = jnp.sqrt(jnp.sum(image_one * image_one) / width + 1e-06)
    first_step = (image_one - energy * initial) / spread
    image_two = apply_operator(first_step, left_ops, right_ops, coefficient, sector_mask)
    chebyshev = 2.0 * (image_two - energy * first_step) / spread - initial
    half_turn = jnp.einsum('kab,bj->kaj', left_ops, basis_rotation, precision=HIGH)
    rotated = jnp.einsum('ai,kaj->kij', basis_rotation, half_turn, precision=HIGH)
    return (chebyshev, energy, rotated)

def reference(left_ops, right_ops, wavefunction, basis_rotation, pair_term, coupling, left_charge, right_charge):
    copies = jnp.broadcast_to(coupling[None, :], (left_ops.shape[0], coupling.shape[0]))
    chebyshev, energy, rotated = lax.map(one_segment, (left_ops, right_ops, wavefunction, basis_rotation, pair_term, copies, left_charge, right_charge))
    handed = jnp.concatenate([left_ops[0:1], rotated[:-1]], axis=0)
    return (chebyshev, energy, handed)
```

```python
import functools
import jax
import jax.numpy as jnp
from jax import lax
from jax.experimental import pallas as pl
from jax.experimental.pallas import tpu as pltpu
from jax.sharding import PartitionSpec as P

MESH = pl.DeviceIdType.MESH
F32, BF16 = jnp.float32, jnp.bfloat16
NX, NZ = 4, 8
SECTORS = 3
M = 768
Q = M // SECTORS
ROWS = 8
OPS = NX * NZ
NN = (((1,), (0,)), ((), ()))
NT = (((1,), (1,)), ((), ()))


def dot(a, b, dims=NN):
    return lax.dot_general(a, b, dims, preferred_element_type=F32)


def dot3(a_high, a_low, b_high, b_low):
    return dot(a_high, b_high) + (dot(a_high, b_low) + dot(a_low, b_high))


def halves(value):
    high = value.astype(BF16)
    low = (value - high.astype(F32)).astype(BF16)
    return high, low


def thirds(value):
    high = value.astype(BF16)
    rest = value - high.astype(F32)
    middle = rest.astype(BF16)
    low = (rest - middle.astype(F32)).astype(BF16)
    return high, middle, low


def peer(dx, dz):
    op = lax.axis_index("op")
    x, z = op // NZ, op % NZ
    return lax.rem(x + dx, NX) * NZ + lax.rem(z + dz, NZ)


def remote(source, target, send, receive, device):
    copy = pltpu.make_async_remote_copy(
        source, target, send, receive, device_id=device, device_id_type=MESH
    )
    copy.start()
    return copy


def kernel(
    left_hbm, right_hbm, basis_hbm, wave_ref, left_charge_ref, right_charge_ref, term_ref, coupling_ref,
    cheb_ref, energy_ref, handed_hbm,
    left, right, basis, load_sem,
    left_high, left_low, right_high, right_low,
    basis_high, basis_low, turned_high, turned_low, half_high, half_low, rotated,
    to_left, to_right, from_left, position_column,
    scratch_high, scratch_low, y_high, y_low, x_high, x_low,
    initial, first, gather_one, gather_two, partial_one, partial_two,
    land_one, land_two, middle_one, middle_two, final_one, final_two,
    send_sems, recv_sems, hand_send, hand_recv, own_sem,
):
    seg, op = lax.axis_index("seg"), lax.axis_index("op")
    x, z = op // NZ, op % NZ
    width = float(M * M)

    loads = [
        pltpu.make_async_copy(source, target, load_sem.at[i])
        for i, (source, target) in enumerate(((right_hbm, right), (left_hbm, left), (basis_hbm, basis)))
    ]
    for load in loads:
        load.start()
    barrier = pltpu.get_barrier_semaphore()
    for dx in range(1, NX):
        pl.semaphore_signal(barrier, inc=1, device_id={"op": peer(dx, 0)}, device_id_type=MESH)
    for dz in range(1, NZ):
        pl.semaphore_signal(barrier, inc=1, device_id={"op": peer(0, dz)}, device_id_type=MESH)
    segs = lax.axis_size("seg")
    for ds in (1, segs - 1):
        pl.semaphore_signal(barrier, inc=1, device_id={"seg": lax.rem(seg + ds, segs)}, device_id_type=MESH)

    before = lax.broadcasted_iota(jnp.int32, (M, M), 0) < lax.broadcasted_iota(jnp.int32, (M, M), 1)
    to_left[...] = jnp.where(before, 1.0, 0.0).astype(BF16)
    sector = lax.broadcasted_iota(jnp.int32, (8, M), 0)
    left_hits = jnp.where(left_charge_ref[...] == sector, 1.0, 0.0)
    right_hits = jnp.where(right_charge_ref[...] == sector, 1.0, 0.0)
    counts = dot(jnp.concatenate([left_hits, right_hits], 0).astype(BF16), to_left[...])
    left_rank = jnp.sum(left_hits * counts[:8], 0, keepdims=True)
    right_rank = jnp.sum(right_hits * counts[8:], 0, keepdims=True)
    left_place = left_charge_ref[...] * Q + left_rank.astype(jnp.int32)
    right_place = right_charge_ref[...] * Q + right_rank.astype(jnp.int32)
    place = lax.broadcasted_iota(jnp.int32, (M, M), 0)
    to_right[...] = jnp.where(place == right_place, 1.0, 0.0).astype(BF16)
    position_column[...] = jnp.transpose(jnp.broadcast_to(left_place.astype(F32), (128, M)))

    own_position = position_column[pl.ds(pl.multiple_of(op * 24, 8), 24), 0:1]
    moved = sum(dot(part, to_right[...], NT) for part in thirds(wave_ref[...]))
    own_rows = jnp.where(
        own_position < Q, moved[:, :Q], jnp.where(own_position < 2 * Q, moved[:, Q : 2 * Q], moved[:, 2 * Q :])
    )
    for p in range(SECTORS):
        gather_one[p, x, z] = own_rows[p * ROWS : (p + 1) * ROWS]

    pl.semaphore_wait(barrier, NX + NZ)

    def along(axis, phase, p, level, source, target):
        copies = []
        for d in range(1, NX if axis == "x" else NZ):
            far = lax.rem(x + d, NX) if axis == "x" else lax.rem(z + d, NZ)
            device = peer(d, 0) if axis == "x" else peer(0, d)
            copies.append(
                remote(
                    source(far), target(d),
                    send_sems.at[phase, p, level, d], recv_sems.at[phase, p, level, d], {"op": device},
                )
            )
        return copies

    sent = []

    def arrived(copies):
        for copy in copies:
            copy.wait_recv()
        sent.extend(copies)

    def gather_near(phase, buffer, p):
        ref = buffer.at[p, x, z]
        return along("x" if p == 0 else "z", phase, p, 0, lambda far: ref, lambda d: ref)

    def gather_far(phase, buffer, p):
        ref = buffer.at[p, :, z] if p == 0 else buffer.at[p, x]
        return along("z" if p == 0 else "x", phase, p, 1, lambda far: ref, lambda d: ref)

    def scatter_far(phase, partial, land, p):
        if p == 0:
            return along("z", phase, p, 0, lambda far: partial.at[p, :, far], lambda d: land[0].at[d])
        return along("x", phase, p, 0, lambda far: partial.at[p, far], lambda d: land[1].at[p - 1, d])

    def scatter_near(phase, partial, land, middle, final, p):
        if p == 0:
            middle[0][...] = partial[p, :, z] + sum(land[0][d] for d in range(1, NZ))
            return along("x", phase, p, 1, lambda far: middle[0].at[far], lambda d: final[0].at[d])
        middle[1][p - 1] = partial[p, x] + sum(land[1][p - 1, d] for d in range(1, NX))
        return along("z", phase, p, 1, lambda far: middle[1].at[p - 1, far], lambda d: final[1].at[p - 1, d])

    def scattered(middle, final, p):
        if p == 0:
            return middle[0][x] + sum(final[0][d] for d in range(1, NX))
        return middle[1][p - 1, z] + sum(final[1][p - 1, d] for d in range(1, NZ))

    def split(source, high, low):
        @pl.loop(0, SECTORS)
        def _(i):
            rows = pl.ds(pl.multiple_of(i * Q, Q), Q)
            high[rows, :], low[rows, :] = halves(source[rows, :])

    def sort_columns(source, order, high, low):
        @pl.loop(0, SECTORS)
        def _(i):
            rows = pl.ds(pl.multiple_of(i * Q, Q), Q)
            part_high, part_low = halves(source[rows, :])
            high[rows, :] = dot(part_high, order[...], NT).astype(BF16)
            low[rows, :] = dot(part_low, order[...], NT).astype(BF16)

    def sort_rows(order, source_high, source_low, high, low):
        @pl.loop(0, SECTORS)
        def _(i):
            rows = pl.ds(pl.multiple_of(i * Q, Q), Q)
            high[rows, :] = dot(order[rows, :], source_high[...]).astype(BF16)
            low[rows, :] = dot(order[rows, :], source_low[...]).astype(BF16)

    def first_turn():
        @pl.loop(0, SECTORS)
        def _(i):
            rows = pl.ds(pl.multiple_of(i * Q, Q), Q)
            part_high, part_low = halves(left[rows, :])
            value = dot3(part_high, part_low, basis_high[...], basis_low[...])
            half_high[rows, :], half_low[rows, :] = halves(value)

    def second_turn():
        for i in range(SECTORS):
            rows = pl.ds(i * Q, Q)
            rotated[rows, :] = dot3(turned_high[rows, :], turned_low[rows, :], half_high[...], half_low[...])

            @pl.when(seg < segs - 1)
            def _():
                hand(i).start()

    def hand(i):
        rows = pl.ds(i * Q, Q)
        return pltpu.make_async_remote_copy(
            rotated.at[rows, :], handed_hbm.at[rows, :], hand_send.at[i], hand_recv.at[i],
            device_id={"seg": lax.rem(seg + 1, segs)}, device_id_type=MESH,
        )

    def transpose_basis():
        for i in range(M // 128):
            cols = pl.ds(i * 128, 128)
            turned_high[:, cols], turned_low[:, cols] = halves(jnp.transpose(basis[cols, :]))

    coefficient = coupling_ref[term_ref[0, 0]]

    def inner(p):
        rows = pl.ds(p * Q, Q)
        value = coefficient * dot3(left_high[:, rows], left_low[:, rows], x_high[rows, :], x_low[rows, :])
        y_high[:, rows], y_low[:, rows] = halves(value)

    def outer(p):
        rows = pl.ds(p * Q, Q)
        return dot3(y_high[rows, :], y_low[rows, :], right_high[:, rows], right_low[:, rows])

    near = [gather_near(0, gather_one, p) for p in range(SECTORS)]

    to_left[...] = jnp.where(place == left_place, 1.0, 0.0).astype(BF16)
    loads[0].wait()
    sort_columns(right, to_right, scratch_high, scratch_low)

    far = []
    for p in range(SECTORS):
        arrived(near[p])
        far.append(gather_far(0, gather_one, p))

    sort_rows(to_right, scratch_high, scratch_low, right_high, right_low)
    loads[1].wait()

    @pl.when(seg == 0)
    def _():
        pltpu.make_async_copy(left, handed_hbm, own_sem).start()

    sort_columns(left, to_left, scratch_high, scratch_low)
    sort_rows(to_left, scratch_high, scratch_low, left_high, left_low)
    lane = lax.broadcasted_iota(jnp.int32, (M, 128), 1).astype(F32)
    for i in range(M // 128):
        hits = position_column[...] == lane + float(i * 128)
        from_left[:, i * 128 : (i + 1) * 128] = jnp.where(hits, 1.0, 0.0).astype(BF16)

    for p in range(SECTORS):
        arrived(far[p])

    whole = gather_one[...].reshape(SECTORS, OPS, ROWS, Q)
    masked = jnp.stack([whole[p] for p in range(SECTORS)], 1).reshape(M, Q)
    scale = jnp.sqrt(jnp.sum(masked * masked) / width + 1e-06)
    masked_high, masked_low = halves(masked / scale)
    sorted_high = dot(to_left[...], masked_high)
    sorted_low = dot(to_left[...], masked_low)
    x_high[...] = sorted_high.astype(BF16)
    x_low[...] = sorted_low.astype(BF16)
    initial[...] = sorted_high + sorted_low
    own_initial = own_rows / scale

    for p in range(SECTORS):
        inner(p)
    far = []
    for p in range(SECTORS):
        partial_one[p] = outer(p).reshape(NX, NZ, ROWS, Q)
        far.append(scatter_far(1, partial_one, land_one, p))

    loads[2].wait()
    split(basis, basis_high, basis_low)
    first_turn()

    near = [None] * SECTORS
    for p in (1, 0, 2):
        arrived(far[p])
        near[p] = scatter_near(1, partial_one, land_one, middle_one, final_one, p)

    transpose_basis()

    far = [None] * SECTORS
    for p in (1, 0, 2):
        arrived(near[p])
        gather_two[p, x, z] = scattered(middle_one, final_one, p)
        far[p] = gather_near(2, gather_two, p)

    second_turn()

    last = [None] * SECTORS
    for p in (1, 0, 2):
        arrived(far[p])
        last[p] = gather_far(2, gather_two, p)
    for p in range(SECTORS):
        arrived(last[p])

    image = gather_two[...].reshape(M, Q)
    start = initial[...]
    energy = jnp.sum(start * image) / width
    spread = jnp.sqrt(jnp.sum(image * image) / width + 1e-06)
    energy_ref[0] = energy
    step = (image - energy * start) / spread
    first[...] = step
    x_high[...], x_low[...] = halves(step)
    for p in range(SECTORS):
        inner(p)
    for p in range(SECTORS):
        out_high, out_low = halves(outer(p))
        rows = pl.ds(p * Q, Q)
        y_high[rows, 0:Q] = out_high
        y_low[rows, 0:Q] = out_low
    back = dot(from_left[...], y_high[:, 0:Q]) + dot(from_left[...], y_low[:, 0:Q])
    back = back.reshape(OPS, SECTORS, ROWS, Q)
    far = []
    for p in range(SECTORS):
        partial_two[p] = back[:, p].reshape(NX, NZ, ROWS, Q)
        far.append(scatter_far(3, partial_two, land_two, p))

    own_select = jnp.where(
        own_position == lax.broadcasted_iota(jnp.int32, (24, M), 1).astype(F32), 1.0, 0.0
    ).astype(BF16)
    own_step = sum(dot(own_select, part) for part in thirds(first[...]))

    near = [None] * SECTORS
    for p in (1, 0, 2):
        arrived(far[p])
        near[p] = scatter_near(3, partial_two, land_two, middle_two, final_two, p)
    own_image = []
    for p in range(SECTORS):
        arrived(near[p])
        own_image.append(scattered(middle_two, final_two, p))
    own_image = jnp.concatenate(own_image, 0)
    result = 2.0 * (own_image - energy * own_step) / spread - own_initial
    spread_out = jnp.concatenate(
        [
            jnp.where((own_position >= p * Q) & (own_position < (p + 1) * Q), result, 0.0)
            for p in range(SECTORS)
        ],
        1,
    )
    cheb_ref[...] = sum(dot(part, to_right[...]) for part in thirds(spread_out))

    for copy in sent:
        copy.wait_send()

    @pl.when(seg == 0)
    def _():
        pltpu.make_async_copy(left, handed_hbm, own_sem).wait()

    @pl.when(seg < segs - 1)
    def _():
        for i in range(SECTORS):
            hand(i).wait_send()

    @pl.when(seg > 0)
    def _():
        for i in range(SECTORS):
            hand(i).wait_recv()


def per_device(
    left_ops,
    right_ops,
    wavefunction,
    basis_rotation,
    pair_term,
    coupling,
    left_charge,
    right_charge,
):
    vmem, smem, hbm = (
        pl.BlockSpec(memory_space=space) for space in (pltpu.VMEM, pltpu.SMEM, pl.ANY)
    )
    dma = pltpu.SemaphoreType.DMA

    def full(dtype):
        return pltpu.VMEM((M, M), dtype)

    def parts():
        return pltpu.VMEM((SECTORS, NX, NZ, ROWS, Q), F32)

    def tall(dtype):
        return pltpu.VMEM((M, Q), dtype)

    land = [pltpu.VMEM((NZ, NX, ROWS, Q), F32), pltpu.VMEM((2, NX, NZ, ROWS, Q), F32)]
    middle = [pltpu.VMEM((NX, ROWS, Q), F32), pltpu.VMEM((2, NZ, ROWS, Q), F32)]
    final = [pltpu.VMEM((NX, ROWS, Q), F32), pltpu.VMEM((2, NZ, ROWS, Q), F32)]
    cheb, energy, handed = pl.pallas_call(
        kernel,
        name="segment_step",
        out_shape=(
            jax.ShapeDtypeStruct((24, M), F32),
            jax.ShapeDtypeStruct((1,), F32),
            jax.ShapeDtypeStruct((M, M), F32),
        ),
        in_specs=[hbm, hbm, hbm, vmem, vmem, vmem, smem, smem],
        out_specs=(vmem, smem, hbm),
        scratch_shapes=[
            full(F32), full(F32), full(F32), dma((3,)),
            full(BF16), full(BF16), full(BF16), full(BF16),
            full(BF16), full(BF16), full(BF16), full(BF16), full(BF16), full(BF16), full(F32),
            full(BF16), full(BF16), full(BF16), pltpu.VMEM((M, 128), F32),
            full(BF16), full(BF16), full(BF16), full(BF16), tall(BF16), tall(BF16),
            tall(F32), tall(F32), parts(), parts(), parts(), parts(),
            list(land), list(land), list(middle), list(middle), list(final), list(final),
            dma((4, SECTORS, 2, NZ)), dma((4, SECTORS, 2, NZ)), dma((SECTORS,)), dma((SECTORS,)), dma,
        ],
        compiler_params=pltpu.CompilerParams(
            collective_id=0, has_side_effects=True, vmem_limit_bytes=58 * 2**20
        ),
    )(
        left_ops[0, 0], right_ops[0, 0], basis_rotation[0], wavefunction[0],
        left_charge, right_charge, pair_term, coupling,
    )
    return cheb[None], energy, handed[None, None]


def solution(mesh):
    placed = (
        P("seg", "op", None, None),
        P("seg", "op", None, None),
        P("seg", "op", None),
        P("seg", None, None),
        P("seg", "op"),
        P(),
        P("seg", None),
        P("seg", None),
    )
    return jax.shard_map(
        per_device,
        mesh=mesh,
        in_specs=placed,
        out_specs=(P("seg", "op", None), P("seg"), P("seg", "op", None, None)),
        check_vma=False,
    )
```

```python
import functools
import jax
import jax.numpy as jnp
from jax import lax
from jax.experimental import pallas as pl
from jax.experimental.pallas import tpu as pltpu
from jax.sharding import PartitionSpec as P

MESH = pl.DeviceIdType.MESH
F32, BF16 = jnp.float32, jnp.bfloat16
NX, NZ = 4, 8
SECTORS = 3
M = 768
Q = M // SECTORS
ROWS = 8
OPS = NX * NZ
OWN = SECTORS * ROWS
X_FAR = (2, 1, 3)
Z_FAR = (4, 3, 5, 2, 6, 1, 7)
DIRECT = [(dx, dz) for dz in Z_FAR + (0,) for dx in X_FAR + (0,) if (dx, dz) != (0, 0)]
Z_GROUPS = ((4,), (3, 5), (2, 6), (1, 7), (0,))
Z_GROUP = {d: i for i, group in enumerate(Z_GROUPS) for d in group}
ARRIVALS = (("x", (1, 3)), ("z", (1, 7)), ("x", (2,)), ("z", (2, 6)), ("z", (3, 5)), ("z", (4,)))
COPIES = 6
NN = (((1,), (0,)), ((), ()))
NT = (((1,), (1,)), ((), ()))


def dot(a, b, dims=NN):
    return lax.dot_general(a, b, dims, preferred_element_type=F32)


def dot3(a_high, a_low, b_high, b_low):
    return dot(a_high, b_high) + (dot(a_high, b_low) + dot(a_low, b_high))


def halves(value):
    high = value.astype(BF16)
    low = (value - high.astype(F32)).astype(BF16)
    return high, low


def thirds(value):
    high = value.astype(BF16)
    rest = value - high.astype(F32)
    middle = rest.astype(BF16)
    low = (rest - middle.astype(F32)).astype(BF16)
    return high, middle, low


def peer(dx, dz):
    op = lax.axis_index("op")
    x, z = op // NZ, op % NZ
    return lax.rem(x + dx, NX) * NZ + lax.rem(z + dz, NZ)


def third_dot(value, other, dims):
    rows = value.shape[0]
    stacked = dot(jnp.concatenate(thirds(value), 0), other, dims)
    return stacked[:rows] + stacked[rows : 2 * rows] + stacked[2 * rows :]


def kernel(
    left_hbm, right_hbm, basis_hbm, wave_ref, left_charge_ref, right_charge_ref, term_ref, coupling_ref,
    cheb_ref, energy_ref, handed_hbm,
    left, right, basis, load_sem,
    left_high, left_low, right_high, right_low,
    basis_high, basis_low, turned_high, turned_low, half_high, half_low, rotated,
    to_left, to_right, from_left, position_column,
    scratch_high, scratch_low, y_high, y_low, x_high, x_low,
    initial, first, gather_one, gather_two, partial_one, partial_two,
    land_one, land_two, send_sems, recv_sems, hand_send, hand_recv,
):
    seg, op = lax.axis_index("seg"), lax.axis_index("op")
    x, z = op // NZ, op % NZ
    width = float(M * M)
    segs = lax.axis_size("seg")

    loads = [
        pltpu.make_async_copy(source, target, load_sem.at[i])
        for i, (source, target) in enumerate(((right_hbm, right), (left_hbm, left), (basis_hbm, basis)))
    ]
    for load in loads:
        load.start()
    barrier = pltpu.get_barrier_semaphore()
    for dx, dz in DIRECT:
        pl.semaphore_signal(barrier, inc=1, device_id={"op": peer(dx, dz)}, device_id_type=MESH)
    for ds in (1, segs - 1):
        pl.semaphore_signal(barrier, inc=1, device_id={"seg": lax.rem(seg + ds, segs)}, device_id_type=MESH)

    before = lax.broadcasted_iota(jnp.int32, (M, M), 0) < lax.broadcasted_iota(jnp.int32, (M, M), 1)
    to_left[...] = jnp.where(before, 1.0, 0.0).astype(BF16)
    sector = lax.broadcasted_iota(jnp.int32, (8, M), 0)
    left_hits = jnp.where(left_charge_ref[...] == sector, 1.0, 0.0)
    right_hits = jnp.where(right_charge_ref[...] == sector, 1.0, 0.0)
    counts = dot(jnp.concatenate([left_hits, right_hits], 0).astype(BF16), to_left[...])
    left_rank = jnp.sum(left_hits * counts[:8], 0, keepdims=True)
    right_rank = jnp.sum(right_hits * counts[8:], 0, keepdims=True)
    left_place = left_charge_ref[...] * Q + left_rank.astype(jnp.int32)
    right_place = right_charge_ref[...] * Q + right_rank.astype(jnp.int32)
    place = lax.broadcasted_iota(jnp.int32, (M, M), 0)
    to_right[...] = jnp.where(place == right_place, 1.0, 0.0).astype(BF16)
    position_column[...] = jnp.transpose(jnp.broadcast_to(left_place.astype(F32), (128, M)))

    own_position = position_column[pl.ds(pl.multiple_of(op * OWN, 8), OWN), 0:1]
    moved = third_dot(wave_ref[...], to_right[...], NT)
    own_rows = jnp.where(
        own_position < Q, moved[:, :Q], jnp.where(own_position < 2 * Q, moved[:, Q : 2 * Q], moved[:, 2 * Q :])
    )
    for p in range(SECTORS):
        gather_one[p, x, z] = own_rows[p * ROWS : (p + 1) * ROWS]

    pl.semaphore_wait(barrier, len(DIRECT) + 2)

    def copy_of(source, target, sends, recvs, send_at, recv_at, dx=0, dz=1):
        return pltpu.make_async_remote_copy(
            source, target, sends.at[send_at], recvs.at[recv_at],
            device_id={"op": peer(dx, dz)}, device_id_type=MESH,
        )

    def gather(buffer, sends, recvs):
        def send(ref, send_at, recv_at, dx, dz):
            copy_of(ref, ref, sends, recvs, send_at, recv_at, dx, dz).start()

        def whole(send_at, recv_at):
            view = (
                buffer.at[0, 0:3, 0], buffer.at[1:3, 0, 0:7], buffer.at[0, :, 0:7], buffer.at[1:3, 0:3],
            )[send_at]
            return copy_of(view, view, sends, recvs, send_at, recv_at)

        def pass_a(away):
            ref = buffer.at[0, lax.rem(x - away + NX, NX), z]
            for d in Z_FAR:
                send(ref, 2, 6, 0, d)

        def pass_b(away):
            ref = buffer.at[1:3, x, lax.rem(z - away + NZ, NZ)]
            for d in X_FAR:
                send(ref, 3, 7, d, 0)

        def start_a():
            ref = buffer.at[0, x, z]
            for d in X_FAR:
                send(ref, 0, 0 if d == 2 else 1, d, 0)
            pass_a(0)

        def start_b():
            ref = buffer.at[1:3, x, z]
            for d in Z_FAR:
                send(ref, 1, 2 + Z_GROUP[d], 0, d)
            pass_b(0)

        def turn():
            for axis, group in ARRIVALS:
                if axis == "x":
                    view = buffer.at[0, 0 : len(group), 0]
                    copy_of(view, view, sends, recvs, 0, 0 if group == (2,) else 1).wait_recv()
                    for away in group:
                        pass_a(away)
                else:
                    view = buffer.at[1:3, 0, 0 : len(group)]
                    copy_of(view, view, sends, recvs, 1, 2 + Z_GROUP[group[0]]).wait_recv()
                    for away in group:
                        pass_b(away)

        def finish():
            whole(2, 6).wait_recv()
            whole(3, 7).wait_recv()

        def drain():
            for at in range(4):
                whole(at, 0).wait_send()

        return start_a, start_b, turn, finish, drain

    def scatter(partial, land, sends, recvs):
        land_a, land_x, middle, land_z = land

        def start_a():
            for dx, dz in DIRECT:
                ref = partial.at[0, lax.rem(x + dx, NX), lax.rem(z + dz, NZ)]
                copy_of(ref, land_a.at[dx * NZ + dz], sends, recvs, 0, 0, dx, dz).start()

        def start_b(p):
            for dz in Z_FAR + (0,):
                for dx in X_FAR:
                    ref = partial.at[p, lax.rem(x + dx, NX), lax.rem(z + dz, NZ)]
                    copy_of(ref, land_x.at[dz, p - 1, dx - 1], sends, recvs, 1, 2 + Z_GROUP[dz], dx, 0).start()

        def turn():
            for group in Z_GROUPS:
                view = land_x.at[0 : len(group)]
                copy_of(view, view, sends, recvs, 1, 2 + Z_GROUP[group[0]]).wait_recv()
                for dz in group:
                    zt = lax.rem(z + dz, NZ)
                    middle[dz] = partial[1:3, x, zt] + (land_x[dz, :, 0] + land_x[dz, :, 1] + land_x[dz, :, 2])
                    if dz:
                        copy_of(middle.at[dz], land_z.at[dz], sends, recvs, 2, 1, 0, dz).start()

        def whole_a():
            return copy_of(land_a.at[1:OPS], land_a.at[1:OPS], sends, recvs, 0, 0)

        def whole_z():
            return copy_of(land_z.at[1:NZ], land_z.at[1:NZ], sends, recvs, 2, 1)

        def finish_a():
            whole_a().wait_recv()
            return partial[0, x, z] + sum(land_a[dx * NZ + dz] for dx, dz in DIRECT)

        def finish_b():
            whole_z().wait_recv()
            return middle[0] + sum(land_z[dz] for dz in Z_FAR)

        def drain():
            whole_a().wait_send()
            copy_of(land_x, land_x, sends, recvs, 1, 0).wait_send()
            whole_z().wait_send()

        return start_a, start_b, turn, finish_a, finish_b, drain

    def blocks(body):
        @pl.loop(0, SECTORS)
        def _(i):
            body(pl.ds(pl.multiple_of(i * Q, Q), Q))

    def sort_columns(source, order):
        def body(rows):
            part_high, part_low = halves(source[rows, :])
            scratch_high[rows, :] = dot(part_high, order[...], NT).astype(BF16)
            scratch_low[rows, :] = dot(part_low, order[...], NT).astype(BF16)

        blocks(body)

    def sort_rows(order, source, target):
        def body(rows):
            target[rows, :] = dot(order[rows, :], source[...]).astype(BF16)

        blocks(body)

    def split_basis():
        def body(rows):
            basis_high[rows, :], basis_low[rows, :] = halves(basis[rows, :])

        blocks(body)
        for i in range(M // 128):
            cols = pl.ds(i * 128, 128)
            turned_high[:, cols], turned_low[:, cols] = halves(jnp.transpose(basis[cols, :]))

    def first_turn():
        def body(rows):
            part_high, part_low = halves(left[rows, :])
            value = dot3(part_high, part_low, basis_high[...], basis_low[...])
            half_high[rows, :], half_low[rows, :] = halves(value)

        blocks(body)

    def second_turn():
        for i in range(SECTORS):
            rows = pl.ds(i * Q, Q)
            rotated[rows, :] = dot3(turned_high[rows, :], turned_low[rows, :], half_high[...], half_low[...])

            @pl.when(seg < segs - 1)
            def _():
                hand(i).start()

    def hand(i):
        rows = pl.ds(i * Q, Q)
        return pltpu.make_async_remote_copy(
            rotated.at[rows, :], handed_hbm.at[rows, :], hand_send.at[i], hand_recv.at[i],
            device_id={"seg": lax.rem(seg + 1, segs)}, device_id_type=MESH,
        )

    coefficient = coupling_ref[term_ref[0, 0]]

    def inner(p):
        rows = pl.ds(p * Q, Q)
        value = coefficient * dot3(left_high[:, rows], left_low[:, rows], x_high[rows, :], x_low[rows, :])
        y_high[:, rows], y_low[:, rows] = halves(value)

    def outer(p):
        rows = pl.ds(p * Q, Q)
        return dot3(y_high[rows, :], y_low[rows, :], right_high[:, rows], right_low[:, rows])

    start_a, start_b, turn, finish, drain_one = gather(gather_one, send_sems[0], recv_sems[0])
    start_b()
    start_a()
    to_left[...] = jnp.where(place == left_place, 1.0, 0.0).astype(BF16)
    loads[0].wait()
    sort_columns(right, to_right)
    sort_rows(to_right, scratch_high, right_high)
    turn()
    sort_rows(to_right, scratch_low, right_low)
    loads[1].wait()
    sort_columns(left, to_left)
    sort_rows(to_left, scratch_high, left_high)
    sort_rows(to_left, scratch_low, left_low)
    finish()

    whole = gather_one[...].reshape(SECTORS, OPS, ROWS, Q)
    masked = jnp.stack([whole[p] for p in range(SECTORS)], 1).reshape(M, Q)
    scale = jnp.sqrt(jnp.sum(masked * masked) / width + 1e-06)
    masked_high, masked_low = halves(masked / scale)
    sorted_high = dot(to_left[...], masked_high)
    sorted_low = dot(to_left[...], masked_low)
    x_high[...] = sorted_high.astype(BF16)
    x_low[...] = sorted_low.astype(BF16)
    initial[...] = sorted_high + sorted_low
    own_initial = own_rows / scale

    for p in range(SECTORS):
        inner(p)
    start_a, start_b, turn, finish_a, finish_b, drain_two = scatter(
        partial_one, land_one, send_sems[1], recv_sems[1]
    )
    for p in (1, 2, 0):
        partial_one[p] = outer(p).reshape(NX, NZ, ROWS, Q)
        if p:
            start_b(p)
        else:
            start_a()

    loads[2].wait()
    split_basis()
    first_turn()
    turn()
    second_turn()
    gather_a, gather_b, turn, finish, drain_three = gather(gather_two, send_sems[2], recv_sems[2])
    gather_two[0, x, z] = finish_a()
    gather_a()
    gather_two[1:3, x, z] = finish_b()
    gather_b()

    lane = lax.broadcasted_iota(jnp.int32, (M, 128), 1).astype(F32)
    for i in range(M // 128):
        hits = position_column[...] == lane + float(i * 128)
        from_left[:, i * 128 : (i + 1) * 128] = jnp.where(hits, 1.0, 0.0).astype(BF16)
    turn()
    finish()

    image = gather_two[...].reshape(M, Q)
    start = initial[...]
    energy = jnp.sum(start * image) / width
    spread = jnp.sqrt(jnp.sum(image * image) / width + 1e-06)
    energy_ref[0] = energy
    step = (image - energy * start) / spread
    first[...] = step
    x_high[...], x_low[...] = halves(step)
    for p in range(SECTORS):
        inner(p)
    for p in range(SECTORS):
        out_high, out_low = halves(outer(p))
        rows = pl.ds(p * Q, Q)
        y_high[rows, 0:Q] = out_high
        y_low[rows, 0:Q] = out_low
    back = dot(from_left[...], y_high[:, 0:Q]) + dot(from_left[...], y_low[:, 0:Q])
    back = back.reshape(OPS, SECTORS, ROWS, Q)
    start_a, start_b, turn, finish_a, finish_b, drain_four = scatter(
        partial_two, land_two, send_sems[3], recv_sems[3]
    )
    for p in (1, 2, 0):
        partial_two[p] = back[:, p].reshape(NX, NZ, ROWS, Q)
        if p:
            start_b(p)
        else:
            start_a()

    own_select = jnp.where(
        own_position == lax.broadcasted_iota(jnp.int32, (OWN, M), 1).astype(F32), 1.0, 0.0
    ).astype(BF16)
    own_step = sum(dot(own_select, part) for part in thirds(first[...]))
    turn()
    own_image = jnp.concatenate([finish_a(), finish_b().reshape(2 * ROWS, Q)], 0)
    result = 2.0 * (own_image - energy * own_step) / spread - own_initial
    spread_out = jnp.concatenate(
        [
            jnp.where((own_position >= p * Q) & (own_position < (p + 1) * Q), result, 0.0)
            for p in range(SECTORS)
        ],
        1,
    )
    cheb_ref[...] = third_dot(spread_out, to_right[...], NN)

    for drain in (drain_one, drain_two, drain_three, drain_four):
        drain()

    @pl.when(seg < segs - 1)
    def _():
        for i in range(SECTORS):
            hand(i).wait_send()

    @pl.when(seg > 0)
    def _():
        for i in range(SECTORS):
            hand(i).wait_recv()


def place_results(cheb_raw, energy_raw, handed_raw, left_hbm, cheb_ref, energy_ref, handed_hbm, held, in_sems, out_sems):
    energy_ref[0] = energy_raw[0]
    cheb_ref[...] = cheb_raw[...]
    rows = M // COPIES

    def fetch(source, i):
        part = pl.ds(i * rows, rows)
        return pltpu.make_async_copy(source.at[part, :], held.at[part, :], in_sems.at[i])

    def put(i):
        part = pl.ds(i * rows, rows)
        return pltpu.make_async_copy(held.at[part, :], handed_hbm.at[part, :], out_sems.at[i])

    @pl.when(lax.axis_index("seg") == 0)
    def _():
        for i in range(COPIES):
            fetch(left_hbm, i).start()

    @pl.when(lax.axis_index("seg") > 0)
    def _():
        for i in range(COPIES):
            fetch(handed_raw, i).start()

    for i in range(COPIES):
        fetch(handed_raw, i).wait()
        put(i).start()
    for i in range(COPIES):
        put(i).wait()


def per_device(
    left_ops,
    right_ops,
    wavefunction,
    basis_rotation,
    pair_term,
    coupling,
    left_charge,
    right_charge,
):
    vmem, smem, hbm = (
        pl.BlockSpec(memory_space=space) for space in (pltpu.VMEM, pltpu.SMEM, pl.ANY)
    )
    dma = pltpu.SemaphoreType.DMA

    def full(dtype):
        return pltpu.VMEM((M, M), dtype)

    def parts():
        return pltpu.VMEM((SECTORS, NX, NZ, ROWS, Q), F32)

    def tall(dtype):
        return pltpu.VMEM((M, Q), dtype)

    land = [
        pltpu.VMEM((OPS, ROWS, Q), F32), pltpu.VMEM((NZ, 2, NX - 1, ROWS, Q), F32),
        pltpu.VMEM((NZ, 2, ROWS, Q), F32), pltpu.VMEM((NZ, 2, ROWS, Q), F32),
    ]
    results = (
        jax.ShapeDtypeStruct((OWN, M), F32),
        jax.ShapeDtypeStruct((1,), F32),
        jax.ShapeDtypeStruct((M, M), F32),
    )
    own_left = left_ops[0, 0]
    cheb, energy, handed = pl.pallas_call(
        kernel,
        name="segment_step",
        out_shape=results,
        in_specs=[hbm, hbm, hbm, vmem, vmem, vmem, smem, smem],
        out_specs=(vmem, smem, hbm),
        scratch_shapes=[
            full(F32), full(F32), full(F32), dma((3,)),
            full(BF16), full(BF16), full(BF16), full(BF16),
            full(BF16), full(BF16), full(BF16), full(BF16), full(BF16), full(BF16), full(F32),
            full(BF16), full(BF16), full(BF16), pltpu.VMEM((M, 128), F32),
            full(BF16), full(BF16), full(BF16), full(BF16), tall(BF16), tall(BF16),
            tall(F32), tall(F32), parts(), parts(), parts(), parts(),
            list(land), list(land),
            [dma((4,)), dma((3,)), dma((4,)), dma((3,))], [dma((8,)), dma((7,)), dma((8,)), dma((7,))], dma((SECTORS,)), dma((SECTORS,)),
        ],
        compiler_params=pltpu.CompilerParams(
            collective_id=0, has_side_effects=True, vmem_limit_bytes=58 * 2**20
        ),
    )(
        own_left, right_ops[0, 0], basis_rotation[0], wavefunction[0],
        left_charge, right_charge, pair_term, coupling,
    )
    cheb, energy, handed = pl.pallas_call(
        place_results,
        name="place_results",
        out_shape=results,
        in_specs=[vmem, smem, hbm, hbm],
        out_specs=(vmem, smem, hbm),
        scratch_shapes=[full(F32), dma((COPIES,)), dma((COPIES,))],
    )(cheb, energy, handed, own_left)
    return cheb[None], energy, handed[None, None]


def solution(mesh):
    placed = (
        P("seg", "op", None, None),
        P("seg", "op", None, None),
        P("seg", "op", None),
        P("seg", None, None),
        P("seg", "op"),
        P(),
        P("seg", None),
        P("seg", None),
    )
    return jax.shard_map(
        per_device,
        mesh=mesh,
        in_specs=placed,
        out_specs=(P("seg", "op", None), P("seg"), P("seg", "op", None, None)),
        check_vma=False,
    )
```

```python
import functools
import jax
import jax.numpy as jnp
from jax import lax
from jax.experimental import pallas as pl
from jax.experimental.pallas import tpu as pltpu
from jax.sharding import PartitionSpec as P

MESH = pl.DeviceIdType.MESH
F32, BF16 = jnp.float32, jnp.bfloat16
NX, NZ = 4, 8
SECTORS = 3
M = 768
Q = M // SECTORS
ROWS = 8
HALF = 128
PARTS = 2 * SECTORS
OPS = NX * NZ
OWN = SECTORS * ROWS
X_FAR = (2, 1, 3)
Z_FAR = (4, 3, 5, 2, 6, 1, 7)
DIRECT = [(dx, dz) for dz in Z_FAR + (0,) for dx in X_FAR + (0,) if (dx, dz) != (0, 0)]
Z_GROUPS = ((4,), (3, 5), (2, 6), (1, 7), (0,))
Z_GROUP = {d: i for i, group in enumerate(Z_GROUPS) for d in group}
CROSS = [(dx, 0) for dx in X_FAR] + [(0, dz) for dz in Z_FAR]
ARRIVALS = (("x", (1, 3)), ("z", (1, 7)), ("x", (2,)), ("z", (2, 6)), ("z", (3, 5)), ("z", (4,)))
NN = (((1,), (0,)), ((), ()))
NT = (((1,), (1,)), ((), ()))


def dot(a, b, dims=NN):
    return lax.dot_general(a, b, dims, preferred_element_type=F32)


def dot3(a_high, a_low, b_high, b_low):
    return dot(a_high, b_high) + (dot(a_high, b_low) + dot(a_low, b_high))


def halves(value):
    high = value.astype(BF16)
    low = (value - high.astype(F32)).astype(BF16)
    return high, low


def thirds(value):
    high = value.astype(BF16)
    rest = value - high.astype(F32)
    middle = rest.astype(BF16)
    low = (rest - middle.astype(F32)).astype(BF16)
    return high, middle, low


def peer(dx, dz):
    op = lax.axis_index("op")
    x, z = op // NZ, op % NZ
    return lax.rem(x + dx, NX) * NZ + lax.rem(z + dz, NZ)


def third_dot(value, other, dims):
    rows = value.shape[0]
    stacked = dot(jnp.concatenate(thirds(value), 0), other, dims)
    return stacked[:rows] + stacked[rows : 2 * rows] + stacked[2 * rows :]


def kernel(
    left_hbm, right_hbm, basis_hbm, wave_hbm, left_charge_hbm, right_charge_hbm, term_hbm, coupling_hbm,
    cheb_ref, energy_ref, handed_ref,
    left, right, basis, wave_ref, left_charge_ref, right_charge_ref, term_ref, coupling_ref, load_sem,
    left_high, left_low, right_high, right_low,
    basis_high, basis_low, turned_high, turned_low, half_high, half_low, rotated,
    to_left, to_right, from_left, position_column,
    scratch_high, scratch_low, y_high, y_low, x_high, x_low,
    initial, first, gather_one, gather_two, partial_one, partial_two,
    land_one, land_two, send_sems, recv_sems, hand_send, hand_recv,
):
    seg, op = lax.axis_index("seg"), lax.axis_index("op")
    x, z = op // NZ, op % NZ
    width = float(M * M)
    segs = lax.axis_size("seg")

    loads = [
        pltpu.make_async_copy(source, target, load_sem.at[i])
        for i, (source, target) in enumerate(
            (
                (right_charge_hbm, right_charge_ref), (left_charge_hbm, left_charge_ref), (wave_hbm, wave_ref),
                (right_hbm, right), (left_hbm, left), (basis_hbm, basis),
                (term_hbm, term_ref), (coupling_hbm, coupling_ref),
            )
        )
    ]
    for load in loads[:3]:
        load.start()
    barrier = pltpu.get_barrier_semaphore()
    for dx, dz in CROSS:
        pl.semaphore_signal(barrier, inc=1, device_id={"op": peer(dx, dz)}, device_id_type=MESH)
    for ds in (1, segs - 1):
        pl.semaphore_signal(barrier, inc=1, device_id={"seg": lax.rem(seg + ds, segs)}, device_id_type=MESH)

    for load in loads[3:]:
        load.start()
    kept = pltpu.make_async_copy(left_hbm, handed_ref, load_sem.at[8])

    @pl.when(seg == 0)
    def _():
        kept.start()

    before = lax.broadcasted_iota(jnp.int32, (M, M), 0) < lax.broadcasted_iota(jnp.int32, (M, M), 1)
    to_left[...] = jnp.where(before, 1.0, 0.0).astype(BF16)
    sector = lax.broadcasted_iota(jnp.int32, (8, M), 0)
    loads[0].wait()
    loads[1].wait()
    left_hits = jnp.where(left_charge_ref[...] == sector, 1.0, 0.0)
    right_hits = jnp.where(right_charge_ref[...] == sector, 1.0, 0.0)
    counts = dot(jnp.concatenate([left_hits, right_hits], 0).astype(BF16), to_left[...])
    left_rank = jnp.sum(left_hits * counts[:8], 0, keepdims=True)
    right_rank = jnp.sum(right_hits * counts[8:], 0, keepdims=True)
    left_place = left_charge_ref[...] * Q + left_rank.astype(jnp.int32)
    right_place = right_charge_ref[...] * Q + right_rank.astype(jnp.int32)
    place = lax.broadcasted_iota(jnp.int32, (M, M), 0)
    to_right[...] = jnp.where(place == right_place, 1.0, 0.0).astype(BF16)
    position_column[...] = jnp.transpose(jnp.broadcast_to(left_place.astype(F32), (128, M)))

    own_position = position_column[pl.ds(pl.multiple_of(op * OWN, 8), OWN), 0:1]
    loads[2].wait()
    moved = third_dot(wave_ref[...], to_right[...], NT)
    own_rows = jnp.where(
        own_position < Q, moved[:, :Q], jnp.where(own_position < 2 * Q, moved[:, Q : 2 * Q], moved[:, 2 * Q :])
    )
    for c in range(PARTS):
        p, cols = c // 2, slice(c % 2 * HALF, (c % 2 + 1) * HALF)
        gather_one[c, x, z] = own_rows[p * ROWS : (p + 1) * ROWS, cols]

    pl.semaphore_wait(barrier, len(CROSS) + 2)

    def copy_of(source, target, sends, recvs, send_at, recv_at, dx=0, dz=1):
        return pltpu.make_async_remote_copy(
            source, target, sends.at[send_at], recvs.at[recv_at],
            device_id={"op": peer(dx, dz)}, device_id_type=MESH,
        )

    def gather(buffer, sends, recvs):
        def send(ref, send_at, recv_at, dx, dz):
            copy_of(ref, ref, sends, recvs, send_at, recv_at, dx, dz).start()

        def whole(send_at, recv_at):
            view = (
                buffer.at[0, 0:3, 0], buffer.at[1:PARTS, 0, 0:7], buffer.at[0, :, 0:7], buffer.at[1:PARTS, 0:3],
            )[send_at]
            return copy_of(view, view, sends, recvs, send_at, recv_at)

        def pass_a(away):
            ref = buffer.at[0, lax.rem(x - away + NX, NX), z]
            for d in Z_FAR:
                send(ref, 2, 6, 0, d)

        def pass_b(away):
            ref = buffer.at[1:PARTS, x, lax.rem(z - away + NZ, NZ)]
            for d in X_FAR:
                send(ref, 3, 7, d, 0)

        def start_a():
            ref = buffer.at[0, x, z]
            for d in X_FAR:
                send(ref, 0, 0 if d == 2 else 1, d, 0)
            pass_a(0)

        def start_b():
            ref = buffer.at[1:PARTS, x, z]
            for d in Z_FAR:
                send(ref, 1, 2 + Z_GROUP[d], 0, d)
            pass_b(0)

        def turn(arrivals):
            for axis, group in arrivals:
                if axis == "x":
                    view = buffer.at[0, 0 : len(group), 0]
                    copy_of(view, view, sends, recvs, 0, 0 if group == (2,) else 1).wait_recv()
                    for away in group:
                        pass_a(away)
                else:
                    view = buffer.at[1:PARTS, 0, 0 : len(group)]
                    copy_of(view, view, sends, recvs, 1, 2 + Z_GROUP[group[0]]).wait_recv()
                    for away in group:
                        pass_b(away)

        def finish():
            whole(2, 6).wait_recv()
            whole(3, 7).wait_recv()

        def drain():
            for at in range(4):
                whole(at, 0).wait_send()

        return start_a, start_b, turn, finish, drain

    def scatter(partial, land, sends, recvs):
        land_a, land_x, middle, land_z = land

        def start_a():
            for dx, dz in DIRECT:
                ref = partial.at[0, lax.rem(x + dx, NX), lax.rem(z + dz, NZ)]
                copy_of(ref, land_a.at[dx * NZ + dz], sends, recvs, 0, 0, dx, dz).start()

        def start_b():
            for dz in Z_FAR + (0,):
                for dx in X_FAR:
                    ref = partial.at[1:PARTS, lax.rem(x + dx, NX), lax.rem(z + dz, NZ)]
                    copy_of(ref, land_x.at[dz, dx - 1], sends, recvs, 1, 2 + Z_GROUP[dz], dx, 0).start()

        def turn(groups):
            for group in groups:
                view = land_x.at[0 : len(group)]
                copy_of(view, view, sends, recvs, 1, 2 + Z_GROUP[group[0]]).wait_recv()
                for dz in group:
                    own = partial[1:PARTS, x, lax.rem(z + dz, NZ)]
                    middle[dz] = own + (land_x[dz, 0] + land_x[dz, 1] + land_x[dz, 2])
                    if dz:
                        copy_of(middle.at[dz], land_z.at[dz], sends, recvs, 2, 1, 0, dz).start()

        def whole_a():
            return copy_of(land_a.at[1:OPS], land_a.at[1:OPS], sends, recvs, 0, 0)

        def whole_z():
            return copy_of(land_z.at[1:NZ], land_z.at[1:NZ], sends, recvs, 2, 1)

        def finish_a():
            whole_a().wait_recv()
            return partial[0, x, z] + sum(land_a[dx * NZ + dz] for dx, dz in DIRECT)

        def finish_b():
            whole_z().wait_recv()
            return middle[0] + sum(land_z[dz] for dz in Z_FAR)

        def drain():
            whole_a().wait_send()
            copy_of(land_x, land_x, sends, recvs, 1, 0).wait_send()
            whole_z().wait_send()

        return start_a, start_b, turn, finish_a, finish_b, drain

    def blocks(body):
        for i in range(SECTORS):
            body(pl.ds(i * Q, Q))

    def sort_columns(source, order):
        def body(rows):
            part_high, part_low = halves(source[rows, :])
            scratch_high[rows, :] = dot(part_high, order[...], NT).astype(BF16)
            scratch_low[rows, :] = dot(part_low, order[...], NT).astype(BF16)

        blocks(body)

    def sort_rows(order, source, target):
        def body(rows):
            target[rows, :] = dot(order[rows, :], source[...]).astype(BF16)

        blocks(body)

    def split_basis():
        def body(rows):
            basis_high[rows, :], basis_low[rows, :] = halves(basis[rows, :])

        blocks(body)
        for i in range(M // 128):
            cols = pl.ds(i * 128, 128)
            turned_high[:, cols], turned_low[:, cols] = halves(jnp.transpose(basis[cols, :]))

    def first_turn():
        def body(rows):
            part_high, part_low = halves(left[rows, :])
            value = dot3(part_high, part_low, basis_high[...], basis_low[...])
            half_high[rows, :], half_low[rows, :] = halves(value)

        blocks(body)

    def second_turn(steps):
        for i in steps:
            rows = pl.ds(i * Q, Q)
            rotated[rows, :] = dot3(turned_high[rows, :], turned_low[rows, :], half_high[...], half_low[...])

            @pl.when(seg < segs - 1)
            def _():
                hand(i).start()

    def hand(i):
        rows = pl.ds(i * Q, Q)
        return pltpu.make_async_remote_copy(
            rotated.at[rows, :], handed_ref.at[rows, :], hand_send.at[i], hand_recv.at[i],
            device_id={"seg": lax.rem(seg + 1, segs)}, device_id_type=MESH,
        )

    def keep(partial, p, value):
        partial[2 * p] = value[:, :HALF].reshape(NX, NZ, ROWS, HALF)
        partial[2 * p + 1] = value[:, HALF:].reshape(NX, NZ, ROWS, HALF)

    def blocks_of(buffer, p):
        return jnp.concatenate([buffer[c].reshape(Q, HALF) for c in (2 * p, 2 * p + 1)], 1)


    def inner(p):
        rows = pl.ds(p * Q, Q)
        value = coefficient * dot3(left_high[:, rows], left_low[:, rows], x_high[rows, :], x_low[rows, :])
        y_high[:, rows], y_low[:, rows] = halves(value)

    def outer(p):
        rows = pl.ds(p * Q, Q)
        return dot3(y_high[rows, :], y_low[rows, :], right_high[:, rows], right_low[:, rows])

    start_a, start_b, turn, finish, drain_one = gather(gather_one, send_sems[0], recv_sems[0])
    start_b()
    start_a()
    to_left[...] = jnp.where(place == left_place, 1.0, 0.0).astype(BF16)
    loads[3].wait()
    sort_columns(right, to_right)
    sort_rows(to_right, scratch_high, right_high)
    turn(ARRIVALS[:2])
    sort_rows(to_right, scratch_low, right_low)
    turn(ARRIVALS[2:])
    loads[4].wait()
    sort_columns(left, to_left)
    sort_rows(to_left, scratch_high, left_high)
    sort_rows(to_left, scratch_low, left_low)
    finish()

    loads[6].wait()
    loads[7].wait()
    coefficient = coupling_ref[term_ref[0, 0]]
    masked = jnp.stack([blocks_of(gather_one, p).reshape(OPS, ROWS, Q) for p in range(SECTORS)], 1).reshape(M, Q)
    scale = jnp.sqrt(jnp.sum(masked * masked) / width + 1e-06)
    masked_high, masked_low = halves(masked / scale)
    sorted_high = dot(to_left[...], masked_high)
    sorted_low = dot(to_left[...], masked_low)
    x_high[...] = sorted_high.astype(BF16)
    x_low[...] = sorted_low.astype(BF16)
    initial[...] = sorted_high + sorted_low
    own_initial = own_rows / scale

    for p in range(SECTORS):
        inner(p)
    start_a, start_b, turn, finish_a, finish_b, drain_two = scatter(
        partial_one, land_one, send_sems[1], recv_sems[1]
    )
    for p in range(SECTORS):
        keep(partial_one, p, outer(p))
    start_b()
    start_a()

    loads[5].wait()
    split_basis()
    first_turn()
    turn(Z_GROUPS[:2])
    second_turn((0,))
    turn(Z_GROUPS[2:4])
    second_turn((1,))
    turn(Z_GROUPS[4:])
    gather_a, gather_b, turn, finish, drain_three = gather(gather_two, send_sems[2], recv_sems[2])
    gather_two[0, x, z] = finish_a()
    gather_a()
    second_turn((2,))
    gather_two[1:PARTS, x, z] = finish_b()
    gather_b()

    lane = lax.broadcasted_iota(jnp.int32, (M, 128), 1).astype(F32)
    by_part = position_column[...].reshape(OPS, SECTORS, ROWS, 128)
    by_part = jnp.concatenate([by_part[:, p].reshape(Q, 128) for p in range(SECTORS)], 0)
    for i in range(M // 128):
        hits = by_part == lane + float(i * 128)
        from_left[:, i * 128 : (i + 1) * 128] = jnp.where(hits, 1.0, 0.0).astype(BF16)
    turn(ARRIVALS)
    finish()

    image = jnp.concatenate([blocks_of(gather_two, p) for p in range(SECTORS)], 0)
    start = initial[...]
    energy = jnp.sum(start * image) / width
    spread = jnp.sqrt(jnp.sum(image * image) / width + 1e-06)
    energy_ref[...] = jnp.full((8, 128), energy, F32)
    step = (image - energy * start) / spread
    first[...] = step
    x_high[...], x_low[...] = halves(step)
    for p in range(SECTORS):
        inner(p)
    for p in range(SECTORS):
        out_high, out_low = halves(outer(p))
        rows = pl.ds(p * Q, Q)
        y_high[rows, 0:Q] = out_high
        y_low[rows, 0:Q] = out_low
    start_a, start_b, turn, finish_a, finish_b, drain_four = scatter(
        partial_two, land_two, send_sems[3], recv_sems[3]
    )
    for p in range(SECTORS):
        rows = pl.ds(p * Q, Q)
        back = dot(from_left[rows, :], y_high[:, 0:Q]) + dot(from_left[rows, :], y_low[:, 0:Q])
        keep(partial_two, p, back)
    start_b()
    start_a()

    own_select = jnp.where(
        own_position == lax.broadcasted_iota(jnp.int32, (OWN, M), 1).astype(F32), 1.0, 0.0
    ).astype(BF16)
    own_step = sum(dot(own_select, part) for part in thirds(first[...]))
    turn(Z_GROUPS)
    part, others = finish_a(), finish_b()
    part = [part] + [others[c] for c in range(PARTS - 1)]
    own_image = jnp.concatenate(
        [jnp.concatenate(part[2 * p : 2 * p + 2], 1) for p in range(SECTORS)], 0
    )
    result = 2.0 * (own_image - energy * own_step) / spread - own_initial
    spread_out = jnp.concatenate(
        [
            jnp.where((own_position >= p * Q) & (own_position < (p + 1) * Q), result, 0.0)
            for p in range(SECTORS)
        ],
        1,
    )
    cheb_ref[...] = third_dot(spread_out, to_right[...], NN)

    for drain in (drain_one, drain_two, drain_three, drain_four):
        drain()

    @pl.when(seg < segs - 1)
    def _():
        for i in range(SECTORS):
            hand(i).wait_send()

    @pl.when(seg > 0)
    def _():
        for i in range(SECTORS):
            hand(i).wait_recv()

    @pl.when(seg == 0)
    def _():
        kept.wait()


def per_device(
    left_ops,
    right_ops,
    wavefunction,
    basis_rotation,
    pair_term,
    coupling,
    left_charge,
    right_charge,
):
    vmem, hbm = (pl.BlockSpec(memory_space=space) for space in (pltpu.VMEM, pl.ANY))
    dma = pltpu.SemaphoreType.DMA

    def full(dtype):
        return pltpu.VMEM((M, M), dtype)

    def parts():
        return pltpu.VMEM((PARTS, NX, NZ, ROWS, HALF), F32)

    def tall(dtype):
        return pltpu.VMEM((M, Q), dtype)

    land = [
        pltpu.VMEM((OPS, ROWS, HALF), F32), pltpu.VMEM((NZ, NX - 1, PARTS - 1, ROWS, HALF), F32),
        pltpu.VMEM((NZ, PARTS - 1, ROWS, HALF), F32), pltpu.VMEM((NZ, PARTS - 1, ROWS, HALF), F32),
    ]
    cheb, energy, handed = pl.pallas_call(
        kernel,
        name="segment_step",
        out_shape=(pltpu.VMEM((OWN, M), F32), pltpu.VMEM((8, 128), F32), pltpu.VMEM((M, M), F32)),
        in_specs=[hbm] * 8,
        out_specs=(vmem, vmem, vmem),
        scratch_shapes=[
            full(F32), full(F32), full(F32), pltpu.VMEM((OWN, M), F32),
            pltpu.VMEM((1, M), jnp.int32), pltpu.VMEM((1, M), jnp.int32),
            pltpu.SMEM((1, 1), jnp.int32), pltpu.SMEM((16,), F32), dma((9,)),
            full(BF16), full(BF16), full(BF16), full(BF16),
            full(BF16), full(BF16), full(BF16), full(BF16), full(BF16), full(BF16), full(F32),
            full(BF16), full(BF16), full(BF16), pltpu.VMEM((M, 128), F32),
            full(BF16), full(BF16), full(BF16), full(BF16), tall(BF16), tall(BF16),
            tall(F32), tall(F32), parts(), parts(), parts(), parts(),
            list(land), list(land),
            [dma((4,)), dma((3,)), dma((4,)), dma((3,))], [dma((8,)), dma((7,)), dma((8,)), dma((7,))], dma((SECTORS,)), dma((SECTORS,)),
        ],
        compiler_params=pltpu.CompilerParams(
            collective_id=0, has_side_effects=True, vmem_limit_bytes=57 * 2**20
        ),
    )(
        left_ops[0, 0], right_ops[0, 0], basis_rotation[0], wavefunction[0],
        left_charge, right_charge, pair_term, coupling,
    )
    return cheb[None], energy[0, :1], handed[None, None]


def solution(mesh):
    placed = (
        P("seg", "op", None, None),
        P("seg", "op", None, None),
        P("seg", "op", None),
        P("seg", None, None),
        P("seg", "op"),
        P(),
        P("seg", None),
        P("seg", None),
    )
    return jax.shard_map(
        per_device,
        mesh=mesh,
        in_specs=placed,
        out_specs=(P("seg", "op", None), P("seg"), P("seg", "op", None, None)),
        check_vma=False,
    )
```

```python
import functools
import jax
import jax.numpy as jnp
from jax import lax
from jax.experimental import pallas as pl
from jax.experimental.pallas import tpu as pltpu
from jax.sharding import PartitionSpec as P

MESH = pl.DeviceIdType.MESH
F32, BF16 = jnp.float32, jnp.bfloat16
NX, NZ = 4, 8
SECTORS = 3
M = 768
Q = M // SECTORS
ROWS = 8
HALF = 128
PARTS = 2 * SECTORS
OPS = NX * NZ
OWN = SECTORS * ROWS
X_FAR = (2, 1, 3)
Z_FAR = (4, 3, 5, 2, 6, 1, 7)
DIRECT = [(dx, dz) for dz in Z_FAR + (0,) for dx in X_FAR + (0,) if (dx, dz) != (0, 0)]
Z_GROUPS = ((4,), (3, 5), (2, 6), (1, 7), (0,))
Z_GROUP = {d: i for i, group in enumerate(Z_GROUPS) for d in group}
CROSS = [(dx, 0) for dx in X_FAR] + [(0, dz) for dz in Z_FAR]
ARRIVALS = (("x", (1, 3)), ("z", (1, 7)), ("x", (2,)), ("z", (2, 6)), ("z", (3, 5)), ("z", (4,)))
NN = (((1,), (0,)), ((), ()))
NT = (((1,), (1,)), ((), ()))


def dot(a, b, dims=NN):
    return lax.dot_general(a, b, dims, preferred_element_type=F32)


def dot3(a_high, a_low, b_high, b_low):
    return dot(a_high, b_high) + (dot(a_high, b_low) + dot(a_low, b_high))


def halves(value):
    high = value.astype(BF16)
    low = (value - high.astype(F32)).astype(BF16)
    return high, low


def thirds(value):
    high = value.astype(BF16)
    rest = value - high.astype(F32)
    middle = rest.astype(BF16)
    low = (rest - middle.astype(F32)).astype(BF16)
    return high, middle, low


def peer(dx, dz):
    op = lax.axis_index("op")
    x, z = op // NZ, op % NZ
    return lax.rem(x + dx, NX) * NZ + lax.rem(z + dz, NZ)


def third_dot(value, other, dims):
    rows = value.shape[0]
    stacked = dot(jnp.concatenate(thirds(value), 0), other, dims)
    return stacked[:rows] + stacked[rows : 2 * rows] + stacked[2 * rows :]


def kernel(
    left_hbm, right_hbm, basis_hbm, wave_hbm, left_charge_hbm, right_charge_hbm, term_hbm, coupling_hbm,
    cheb_ref, energy_ref, handed_ref,
    left, right, basis, wave_ref, left_charge_ref, right_charge_ref, term_ref, coupling_ref, load_sem,
    left_high, left_low, right_high, right_low,
    basis_high, basis_low, turned_high, turned_low, half_high, half_low, rotated,
    to_left, to_right, from_left, position_column,
    scratch_high, scratch_low, y_high, y_low, x_high, x_low,
    initial, first, gather_one, gather_two, partial_one, partial_two,
    land_one, land_two, send_sems, recv_sems, hand_send, hand_recv,
):
    seg, op = lax.axis_index("seg"), lax.axis_index("op")
    x, z = op // NZ, op % NZ
    width = float(M * M)
    segs = lax.axis_size("seg")

    loads = [
        pltpu.make_async_copy(source, target, load_sem.at[i])
        for i, (source, target) in enumerate(
            (
                (right_charge_hbm, right_charge_ref), (left_charge_hbm, left_charge_ref), (wave_hbm, wave_ref),
                (right_hbm, right), (left_hbm, left), (basis_hbm, basis),
                (term_hbm, term_ref), (coupling_hbm, coupling_ref),
            )
        )
    ]
    for load in loads[:3]:
        load.start()
    barrier = pltpu.get_barrier_semaphore()
    for dx, dz in CROSS:
        pl.semaphore_signal(barrier, inc=1, device_id={"op": peer(dx, dz)}, device_id_type=MESH)
    for ds in (1, segs - 1):
        pl.semaphore_signal(barrier, inc=1, device_id={"seg": lax.rem(seg + ds, segs)}, device_id_type=MESH)

    for load in loads[3:]:
        load.start()
    kept = pltpu.make_async_copy(left_hbm, handed_ref, load_sem.at[8])

    @pl.when(seg == 0)
    def _():
        kept.start()

    before = lax.broadcasted_iota(jnp.int32, (M, M), 0) < lax.broadcasted_iota(jnp.int32, (M, M), 1)
    to_left[...] = jnp.where(before, 1.0, 0.0).astype(BF16)
    sector = lax.broadcasted_iota(jnp.int32, (8, M), 0)
    loads[0].wait()
    loads[1].wait()
    left_hits = jnp.where(left_charge_ref[...] == sector, 1.0, 0.0)
    right_hits = jnp.where(right_charge_ref[...] == sector, 1.0, 0.0)
    counts = dot(jnp.concatenate([left_hits, right_hits], 0).astype(BF16), to_left[...])
    left_rank = jnp.sum(left_hits * counts[:8], 0, keepdims=True)
    right_rank = jnp.sum(right_hits * counts[8:], 0, keepdims=True)
    left_place = left_charge_ref[...] * Q + left_rank.astype(jnp.int32)
    right_place = right_charge_ref[...] * Q + right_rank.astype(jnp.int32)
    place = lax.broadcasted_iota(jnp.int32, (M, M), 0)
    to_right[...] = jnp.where(place == right_place, 1.0, 0.0).astype(BF16)
    position_column[...] = jnp.transpose(jnp.broadcast_to(left_place.astype(F32), (128, M)))

    own_position = position_column[pl.ds(pl.multiple_of(op * OWN, 8), OWN), 0:1]
    loads[2].wait()
    moved = third_dot(wave_ref[...], to_right[...], NT)
    own_rows = jnp.where(
        own_position < Q, moved[:, :Q], jnp.where(own_position < 2 * Q, moved[:, Q : 2 * Q], moved[:, 2 * Q :])
    )
    for c in range(PARTS):
        p, cols = c // 2, slice(c % 2 * HALF, (c % 2 + 1) * HALF)
        gather_one[c, x, z] = own_rows[p * ROWS : (p + 1) * ROWS, cols]

    def blocks(body):
        for i in range(SECTORS):
            body(pl.ds(i * Q, Q))

    def sort_columns(source, order, which):
        def body(rows):
            part = halves(source[rows, :])[which]
            (scratch_high, scratch_low)[which][rows, :] = dot(part, order[...], NT).astype(BF16)

        blocks(body)

    def sort_rows(order, source, target):
        def body(rows):
            target[rows, :] = dot(order[rows, :], source[...]).astype(BF16)

        blocks(body)

    pl.semaphore_wait(barrier, len(CROSS) + 2)

    def copy_of(source, target, sends, recvs, send_at, recv_at, dx=0, dz=1):
        return pltpu.make_async_remote_copy(
            source, target, sends.at[send_at], recvs.at[recv_at],
            device_id={"op": peer(dx, dz)}, device_id_type=MESH,
        )

    def gather(buffer, sends, recvs):
        def send(ref, send_at, recv_at, dx, dz):
            copy_of(ref, ref, sends, recvs, send_at, recv_at, dx, dz).start()

        def whole(send_at, recv_at):
            view = (
                buffer.at[0, 0:3, 0], buffer.at[1:PARTS, 0, 0:7], buffer.at[0, :, 0:7], buffer.at[1:PARTS, 0:3],
            )[send_at]
            return copy_of(view, view, sends, recvs, send_at, recv_at)

        def pass_a(away):
            ref = buffer.at[0, lax.rem(x - away + NX, NX), z]
            for d in Z_FAR:
                send(ref, 2, 6, 0, d)

        def pass_b(away):
            ref = buffer.at[1:PARTS, x, lax.rem(z - away + NZ, NZ)]
            for d in X_FAR:
                send(ref, 3, 7, d, 0)

        def start_a():
            ref = buffer.at[0, x, z]
            for d in X_FAR:
                send(ref, 0, 0 if d == 2 else 1, d, 0)
            pass_a(0)

        def start_b():
            ref = buffer.at[1:PARTS, x, z]
            for d in Z_FAR:
                send(ref, 1, 2 + Z_GROUP[d], 0, d)
            pass_b(0)

        def turn(arrivals):
            for axis, group in arrivals:
                if axis == "x":
                    view = buffer.at[0, 0 : len(group), 0]
                    copy_of(view, view, sends, recvs, 0, 0 if group == (2,) else 1).wait_recv()
                    for away in group:
                        pass_a(away)
                else:
                    view = buffer.at[1:PARTS, 0, 0 : len(group)]
                    copy_of(view, view, sends, recvs, 1, 2 + Z_GROUP[group[0]]).wait_recv()
                    for away in group:
                        pass_b(away)

        def finish():
            whole(2, 6).wait_recv()
            whole(3, 7).wait_recv()

        def drain():
            for at in range(4):
                whole(at, 0).wait_send()

        return start_a, start_b, turn, finish, drain

    def scatter(partial, land, sends, recvs):
        land_a, land_x, middle, land_z = land

        def start_a():
            for dx, dz in DIRECT:
                ref = partial.at[0, lax.rem(x + dx, NX), lax.rem(z + dz, NZ)]
                copy_of(ref, land_a.at[dx * NZ + dz], sends, recvs, 0, 0, dx, dz).start()

        def start_b():
            for dz in Z_FAR + (0,):
                for dx in X_FAR:
                    ref = partial.at[1:PARTS, lax.rem(x + dx, NX), lax.rem(z + dz, NZ)]
                    copy_of(ref, land_x.at[dz, dx - 1], sends, recvs, 1, 2 + Z_GROUP[dz], dx, 0).start()

        def turn(groups):
            for group in groups:
                view = land_x.at[0 : len(group)]
                copy_of(view, view, sends, recvs, 1, 2 + Z_GROUP[group[0]]).wait_recv()
                for dz in group:
                    own = partial[1:PARTS, x, lax.rem(z + dz, NZ)]
                    middle[dz] = own + (land_x[dz, 0] + land_x[dz, 1] + land_x[dz, 2])
                    if dz:
                        copy_of(middle.at[dz], land_z.at[dz], sends, recvs, 2, 1, 0, dz).start()

        def whole_a():
            return copy_of(land_a.at[1:OPS], land_a.at[1:OPS], sends, recvs, 0, 0)

        def whole_z():
            return copy_of(land_z.at[1:NZ], land_z.at[1:NZ], sends, recvs, 2, 1)

        def finish_a():
            whole_a().wait_recv()
            return partial[0, x, z] + sum(land_a[dx * NZ + dz] for dx, dz in DIRECT)

        def finish_b():
            whole_z().wait_recv()
            return middle[0] + sum(land_z[dz] for dz in Z_FAR)

        def drain():
            whole_a().wait_send()
            copy_of(land_x, land_x, sends, recvs, 1, 0).wait_send()
            whole_z().wait_send()

        return start_a, start_b, turn, finish_a, finish_b, drain

    def split_basis():
        def body(rows):
            basis_high[rows, :], basis_low[rows, :] = halves(basis[rows, :])

        blocks(body)
        for i in range(M // 128):
            cols = pl.ds(i * 128, 128)
            turned_high[:, cols], turned_low[:, cols] = halves(jnp.transpose(basis[cols, :]))

    def first_turn():
        def body(rows):
            part_high, part_low = halves(left[rows, :])
            value = dot3(part_high, part_low, basis_high[...], basis_low[...])
            half_high[rows, :], half_low[rows, :] = halves(value)

        blocks(body)

    def second_turn(steps):
        for i in steps:
            rows = pl.ds(i * Q, Q)
            rotated[rows, :] = dot3(turned_high[rows, :], turned_low[rows, :], half_high[...], half_low[...])

            @pl.when(seg < segs - 1)
            def _():
                hand(i).start()

    def hand(i):
        rows = pl.ds(i * Q, Q)
        return pltpu.make_async_remote_copy(
            rotated.at[rows, :], handed_ref.at[rows, :], hand_send.at[i], hand_recv.at[i],
            device_id={"seg": lax.rem(seg + 1, segs)}, device_id_type=MESH,
        )

    def keep(partial, p, value):
        partial[2 * p] = value[:, :HALF].reshape(NX, NZ, ROWS, HALF)
        partial[2 * p + 1] = value[:, HALF:].reshape(NX, NZ, ROWS, HALF)

    def blocks_of(buffer, p):
        return jnp.concatenate([buffer[c].reshape(Q, HALF) for c in (2 * p, 2 * p + 1)], 1)


    def inner(p):
        rows = pl.ds(p * Q, Q)
        value = coefficient * dot3(left_high[:, rows], left_low[:, rows], x_high[rows, :], x_low[rows, :])
        y_high[:, rows], y_low[:, rows] = halves(value)

    def outer(p):
        rows = pl.ds(p * Q, Q)
        return dot3(y_high[rows, :], y_low[rows, :], right_high[:, rows], right_low[:, rows])

    start_a, start_b, turn, finish, drain_one = gather(gather_one, send_sems[0], recv_sems[0])
    start_b()
    start_a()
    to_left[...] = jnp.where(place == left_place, 1.0, 0.0).astype(BF16)
    loads[3].wait()
    sort_columns(right, to_right, 0)
    sort_columns(right, to_right, 1)
    sort_rows(to_right, scratch_high, right_high)
    turn(ARRIVALS[:2])
    sort_rows(to_right, scratch_low, right_low)
    turn(ARRIVALS[2:])
    loads[4].wait()
    sort_columns(left, to_left, 0)
    sort_columns(left, to_left, 1)
    sort_rows(to_left, scratch_high, left_high)
    sort_rows(to_left, scratch_low, left_low)
    finish()

    loads[6].wait()
    loads[7].wait()
    coefficient = coupling_ref[term_ref[0, 0]]
    masked = jnp.stack([blocks_of(gather_one, p).reshape(OPS, ROWS, Q) for p in range(SECTORS)], 1).reshape(M, Q)
    scale = jnp.sqrt(jnp.sum(masked * masked) / width + 1e-06)
    masked_high, masked_low = halves(masked / scale)
    sorted_high = dot(to_left[...], masked_high)
    sorted_low = dot(to_left[...], masked_low)
    x_high[...] = sorted_high.astype(BF16)
    x_low[...] = sorted_low.astype(BF16)
    initial[...] = sorted_high + sorted_low
    own_initial = own_rows / scale

    for p in range(SECTORS):
        inner(p)
    start_a, start_b, turn, finish_a, finish_b, drain_two = scatter(
        partial_one, land_one, send_sems[1], recv_sems[1]
    )
    for p in range(SECTORS):
        keep(partial_one, p, outer(p))
    start_b()
    start_a()

    loads[5].wait()
    split_basis()
    first_turn()
    turn(Z_GROUPS[:2])
    second_turn((0,))
    turn(Z_GROUPS[2:4])
    second_turn((1,))
    turn(Z_GROUPS[4:])
    gather_a, gather_b, turn, finish, drain_three = gather(gather_two, send_sems[2], recv_sems[2])
    gather_two[0, x, z] = finish_a()
    gather_a()
    gather_two[1:PARTS, x, z] = finish_b()
    gather_b()
    second_turn((2,))

    lane = lax.broadcasted_iota(jnp.int32, (M, 128), 1).astype(F32)
    by_part = position_column[...].reshape(OPS, SECTORS, ROWS, 128)
    by_part = jnp.concatenate([by_part[:, p].reshape(Q, 128) for p in range(SECTORS)], 0)
    for i in range(M // 128):
        hits = by_part == lane + float(i * 128)
        from_left[:, i * 128 : (i + 1) * 128] = jnp.where(hits, 1.0, 0.0).astype(BF16)
    turn(ARRIVALS)
    finish()

    image = jnp.concatenate([blocks_of(gather_two, p) for p in range(SECTORS)], 0)
    start = initial[...]
    energy = jnp.sum(start * image) / width
    spread = jnp.sqrt(jnp.sum(image * image) / width + 1e-06)
    energy_ref[...] = jnp.full((8, 128), energy, F32)
    step = (image - energy * start) / spread
    first[...] = step
    x_high[...], x_low[...] = halves(step)
    for p in range(SECTORS):
        inner(p)
    for p in range(SECTORS):
        out_high, out_low = halves(outer(p))
        rows = pl.ds(p * Q, Q)
        y_high[rows, 0:Q] = out_high
        y_low[rows, 0:Q] = out_low
    start_a, start_b, turn, finish_a, finish_b, drain_four = scatter(
        partial_two, land_two, send_sems[3], recv_sems[3]
    )
    for p in range(SECTORS):
        rows = pl.ds(p * Q, Q)
        back = dot(from_left[rows, :], y_high[:, 0:Q]) + dot(from_left[rows, :], y_low[:, 0:Q])
        keep(partial_two, p, back)
    start_b()
    start_a()

    own_select = jnp.where(
        own_position == lax.broadcasted_iota(jnp.int32, (OWN, M), 1).astype(F32), 1.0, 0.0
    ).astype(BF16)
    own_step = sum(dot(own_select, part) for part in thirds(first[...]))
    turn(Z_GROUPS)
    part, others = finish_a(), finish_b()
    part = [part] + [others[c] for c in range(PARTS - 1)]
    own_image = jnp.concatenate(
        [jnp.concatenate(part[2 * p : 2 * p + 2], 1) for p in range(SECTORS)], 0
    )
    result = 2.0 * (own_image - energy * own_step) / spread - own_initial
    spread_out = jnp.concatenate(
        [
            jnp.where((own_position >= p * Q) & (own_position < (p + 1) * Q), result, 0.0)
            for p in range(SECTORS)
        ],
        1,
    )
    cheb_ref[...] = third_dot(spread_out, to_right[...], NN)

    for drain in (drain_one, drain_two, drain_three, drain_four):
        drain()

    @pl.when(seg < segs - 1)
    def _():
        for i in range(SECTORS):
            hand(i).wait_send()

    @pl.when(seg > 0)
    def _():
        for i in range(SECTORS):
            hand(i).wait_recv()

    @pl.when(seg == 0)
    def _():
        kept.wait()


def per_device(
    left_ops,
    right_ops,
    wavefunction,
    basis_rotation,
    pair_term,
    coupling,
    left_charge,
    right_charge,
):
    vmem, hbm = (pl.BlockSpec(memory_space=space) for space in (pltpu.VMEM, pl.ANY))
    dma = pltpu.SemaphoreType.DMA

    def full(dtype):
        return pltpu.VMEM((M, M), dtype)

    def parts():
        return pltpu.VMEM((PARTS, NX, NZ, ROWS, HALF), F32)

    def tall(dtype):
        return pltpu.VMEM((M, Q), dtype)

    land = [
        pltpu.VMEM((OPS, ROWS, HALF), F32), pltpu.VMEM((NZ, NX - 1, PARTS - 1, ROWS, HALF), F32),
        pltpu.VMEM((NZ, PARTS - 1, ROWS, HALF), F32), pltpu.VMEM((NZ, PARTS - 1, ROWS, HALF), F32),
    ]
    cheb, energy, handed = pl.pallas_call(
        kernel,
        name="segment_step",
        out_shape=(pltpu.VMEM((OWN, M), F32), pltpu.VMEM((8, 128), F32), pltpu.VMEM((M, M), F32)),
        in_specs=[hbm] * 8,
        out_specs=(vmem, vmem, vmem),
        scratch_shapes=[
            full(F32), full(F32), full(F32), pltpu.VMEM((OWN, M), F32),
            pltpu.VMEM((1, M), jnp.int32), pltpu.VMEM((1, M), jnp.int32),
            pltpu.SMEM((1, 1), jnp.int32), pltpu.SMEM((16,), F32), dma((9,)),
            full(BF16), full(BF16), full(BF16), full(BF16),
            full(BF16), full(BF16), full(BF16), full(BF16), full(BF16), full(BF16), full(F32),
            full(BF16), full(BF16), full(BF16), pltpu.VMEM((M, 128), F32),
            full(BF16), full(BF16), full(BF16), full(BF16), tall(BF16), tall(BF16),
            tall(F32), tall(F32), parts(), parts(), parts(), parts(),
            list(land), list(land),
            [dma((4,)), dma((3,)), dma((4,)), dma((3,))], [dma((8,)), dma((7,)), dma((8,)), dma((7,))], dma((SECTORS,)), dma((SECTORS,)),
        ],
        compiler_params=pltpu.CompilerParams(
            collective_id=0, has_side_effects=True, vmem_limit_bytes=57 * 2**20
        ),
    )(
        left_ops[0, 0], right_ops[0, 0], basis_rotation[0], wavefunction[0],
        left_charge, right_charge, pair_term, coupling,
    )
    return cheb[None], energy[0, :1], handed[None, None]


def solution(mesh):
    placed = (
        P("seg", "op", None, None),
        P("seg", "op", None, None),
        P("seg", "op", None),
        P("seg", None, None),
        P("seg", "op"),
        P(),
        P("seg", None),
        P("seg", None),
    )
    return jax.shard_map(
        per_device,
        mesh=mesh,
        in_specs=placed,
        out_specs=(P("seg", "op", None), P("seg"), P("seg", "op", None, None)),
        check_vma=False,
    )
```

```python
import functools
import jax
import jax.numpy as jnp
from jax import lax
from jax.experimental import pallas as pl
from jax.experimental.pallas import tpu as pltpu
from jax.sharding import PartitionSpec as P

MESH = pl.DeviceIdType.MESH
F32, BF16 = jnp.float32, jnp.bfloat16
NX, NZ = 4, 8
SECTORS = 3
M = 768
Q = M // SECTORS
ROWS = 8
HALF = 128
PARTS = 2 * SECTORS
OPS = NX * NZ
OWN = SECTORS * ROWS
X_FAR = (2, 1, 3)
Z_FAR = (4, 3, 5, 2, 6, 1, 7)
DIRECT = [(dx, dz) for dz in Z_FAR + (0,) for dx in X_FAR + (0,) if (dx, dz) != (0, 0)]
Z_GROUPS = ((4,), (3, 5), (2, 6), (1, 7), (0,))
Z_GROUP = {d: i for i, group in enumerate(Z_GROUPS) for d in group}
CROSS = [(dx, 0) for dx in X_FAR] + [(0, dz) for dz in Z_FAR]
ARRIVALS = (("x", (1, 3)), ("z", (1, 7)), ("x", (2,)), ("z", (2, 6)), ("z", (3, 5)), ("z", (4,)))
NN = (((1,), (0,)), ((), ()))
NT = (((1,), (1,)), ((), ()))


def dot(a, b, dims=NN):
    return lax.dot_general(a, b, dims, preferred_element_type=F32)


def dot3(a_high, a_low, b_high, b_low):
    return dot(a_high, b_high) + (dot(a_high, b_low) + dot(a_low, b_high))


def halves(value):
    high = value.astype(BF16)
    low = (value - high.astype(F32)).astype(BF16)
    return high, low


def thirds(value):
    high = value.astype(BF16)
    rest = value - high.astype(F32)
    middle = rest.astype(BF16)
    low = (rest - middle.astype(F32)).astype(BF16)
    return high, middle, low


def peer(dx, dz):
    op = lax.axis_index("op")
    x, z = op // NZ, op % NZ
    return lax.rem(x + dx, NX) * NZ + lax.rem(z + dz, NZ)


def third_dot(value, other, dims):
    rows = value.shape[0]
    stacked = dot(jnp.concatenate(thirds(value), 0), other, dims)
    return stacked[:rows] + stacked[rows : 2 * rows] + stacked[2 * rows :]


def kernel(
    left_hbm, right_hbm, basis_hbm, wave_hbm, left_charge_hbm, right_charge_hbm, term_hbm, coupling_hbm,
    cheb_ref, energy_ref, handed_ref,
    left, right, basis, wave_ref, left_charge_ref, right_charge_ref, term_ref, coupling_ref, load_sem,
    left_high, left_low, right_high, right_low,
    basis_high, basis_low, turned_high, turned_low, half_high, half_low, rotated,
    to_left, to_right, from_left, position_column,
    scratch_high, scratch_low, y_high, y_low, x_high, x_low,
    initial, first, gather_one, gather_two, partial_one, partial_two,
    land_one, land_two, send_sems, recv_sems, hand_send, hand_recv,
):
    seg, op = lax.axis_index("seg"), lax.axis_index("op")
    x, z = op // NZ, op % NZ
    width = float(M * M)
    segs = lax.axis_size("seg")

    loads = [
        pltpu.make_async_copy(source, target, load_sem.at[i])
        for i, (source, target) in enumerate(
            (
                (right_charge_hbm, right_charge_ref), (left_charge_hbm, left_charge_ref), (wave_hbm, wave_ref),
                (right_hbm, right), (left_hbm, left), (basis_hbm, basis),
                (term_hbm, term_ref), (coupling_hbm, coupling_ref),
            )
        )
    ]
    for load in loads[:3]:
        load.start()
    barrier = pltpu.get_barrier_semaphore()
    for dx, dz in CROSS:
        pl.semaphore_signal(barrier, inc=1, device_id={"op": peer(dx, dz)}, device_id_type=MESH)
    for ds in (1, segs - 1):
        pl.semaphore_signal(barrier, inc=1, device_id={"seg": lax.rem(seg + ds, segs)}, device_id_type=MESH)

    for load in loads[3:]:
        load.start()
    kept = pltpu.make_async_copy(left_hbm, handed_ref, load_sem.at[8])

    @pl.when(seg == 0)
    def _():
        kept.start()

    before = lax.broadcasted_iota(jnp.int32, (M, M), 0) < lax.broadcasted_iota(jnp.int32, (M, M), 1)
    to_left[...] = jnp.where(before, 1.0, 0.0).astype(BF16)
    sector = lax.broadcasted_iota(jnp.int32, (8, M), 0)
    loads[0].wait()
    loads[1].wait()
    left_hits = jnp.where(left_charge_ref[...] == sector, 1.0, 0.0)
    right_hits = jnp.where(right_charge_ref[...] == sector, 1.0, 0.0)
    counts = dot(jnp.concatenate([left_hits, right_hits], 0).astype(BF16), to_left[...])
    left_rank = jnp.sum(left_hits * counts[:8], 0, keepdims=True)
    right_rank = jnp.sum(right_hits * counts[8:], 0, keepdims=True)
    left_place = left_charge_ref[...] * Q + left_rank.astype(jnp.int32)
    right_place = right_charge_ref[...] * Q + right_rank.astype(jnp.int32)
    place = lax.broadcasted_iota(jnp.int32, (M, M), 0)
    to_right[...] = jnp.where(place == right_place, 1.0, 0.0).astype(BF16)
    position_column[...] = jnp.transpose(jnp.broadcast_to(left_place.astype(F32), (128, M)))

    own_position = position_column[pl.ds(pl.multiple_of(op * OWN, 8), OWN), 0:1]
    loads[2].wait()
    moved = third_dot(wave_ref[...], to_right[...], NT)
    own_rows = jnp.where(
        own_position < Q, moved[:, :Q], jnp.where(own_position < 2 * Q, moved[:, Q : 2 * Q], moved[:, 2 * Q :])
    )
    for c in range(PARTS):
        p, cols = c // 2, slice(c % 2 * HALF, (c % 2 + 1) * HALF)
        gather_one[c, x, z] = own_rows[p * ROWS : (p + 1) * ROWS, cols]

    def blocks(body):
        for i in range(SECTORS):
            body(pl.ds(i * Q, Q))

    def sort_columns(source, order, which):
        def body(rows):
            part = halves(source[rows, :])[which]
            (scratch_high, scratch_low)[which][rows, :] = dot(part, order[...], NT).astype(BF16)

        blocks(body)

    def sort_rows(order, source, target):
        def body(rows):
            target[rows, :] = dot(order[rows, :], source[...]).astype(BF16)

        blocks(body)

    pl.semaphore_wait(barrier, len(CROSS) + 2)

    def copy_of(source, target, sends, recvs, send_at, recv_at, dx=0, dz=1):
        return pltpu.make_async_remote_copy(
            source, target, sends.at[send_at], recvs.at[recv_at],
            device_id={"op": peer(dx, dz)}, device_id_type=MESH,
        )

    def gather(buffer, sends, recvs):
        def send(ref, send_at, recv_at, dx, dz):
            copy_of(ref, ref, sends, recvs, send_at, recv_at, dx, dz).start()

        def whole(send_at, recv_at):
            view = (
                buffer.at[0, 0:3, 0], buffer.at[1:PARTS, 0, 0:7], buffer.at[0, :, 0:7], buffer.at[1:PARTS, 0:3],
            )[send_at]
            return copy_of(view, view, sends, recvs, send_at, recv_at)

        def pass_a(away):
            ref = buffer.at[0, lax.rem(x - away + NX, NX), z]
            for d in Z_FAR:
                send(ref, 2, 6, 0, d)

        def pass_b(away):
            ref = buffer.at[1:PARTS, x, lax.rem(z - away + NZ, NZ)]
            for d in X_FAR:
                send(ref, 3, 7, d, 0)

        def start_a():
            ref = buffer.at[0, x, z]
            for d in X_FAR:
                send(ref, 0, 0 if d == 2 else 1, d, 0)

        def start_b():
            ref = buffer.at[1:PARTS, x, z]
            for d in Z_FAR:
                send(ref, 1, 2 + Z_GROUP[d], 0, d)

        def turn(arrivals):
            for axis, group in arrivals:
                if axis == "x":
                    view = buffer.at[0, 0 : len(group), 0]
                    copy_of(view, view, sends, recvs, 0, 0 if group == (2,) else 1).wait_recv()
                    for away in group:
                        pass_a(away)
                else:
                    view = buffer.at[1:PARTS, 0, 0 : len(group)]
                    copy_of(view, view, sends, recvs, 1, 2 + Z_GROUP[group[0]]).wait_recv()
                    for away in group:
                        pass_b(away)

        def finish():
            whole(2, 6).wait_recv()
            whole(3, 7).wait_recv()

        def drain():
            for at in range(4):
                whole(at, 0).wait_send()

        return start_a, start_b, pass_a, pass_b, turn, finish, drain

    def scatter(partial, land, sends, recvs):
        land_a, land_x, middle, land_z = land

        def start_a():
            for dx, dz in DIRECT:
                ref = partial.at[0, lax.rem(x + dx, NX), lax.rem(z + dz, NZ)]
                copy_of(ref, land_a.at[dx * NZ + dz], sends, recvs, 0, 0, dx, dz).start()

        def start_b():
            for dz in Z_FAR + (0,):
                for dx in X_FAR:
                    ref = partial.at[1:PARTS, lax.rem(x + dx, NX), lax.rem(z + dz, NZ)]
                    copy_of(ref, land_x.at[dz, dx - 1], sends, recvs, 1, 2 + Z_GROUP[dz], dx, 0).start()

        def turn(groups):
            for group in groups:
                view = land_x.at[0 : len(group)]
                copy_of(view, view, sends, recvs, 1, 2 + Z_GROUP[group[0]]).wait_recv()
                for dz in group:
                    own = partial[1:PARTS, x, lax.rem(z + dz, NZ)]
                    middle[dz] = own + (land_x[dz, 0] + land_x[dz, 1] + land_x[dz, 2])
                    if dz:
                        copy_of(middle.at[dz], land_z.at[dz], sends, recvs, 2, 1, 0, dz).start()

        def whole_a():
            return copy_of(land_a.at[1:OPS], land_a.at[1:OPS], sends, recvs, 0, 0)

        def whole_z():
            return copy_of(land_z.at[1:NZ], land_z.at[1:NZ], sends, recvs, 2, 1)

        def finish_a():
            whole_a().wait_recv()
            return partial[0, x, z] + sum(land_a[dx * NZ + dz] for dx, dz in DIRECT)

        def finish_b():
            whole_z().wait_recv()
            return middle[0] + sum(land_z[dz] for dz in Z_FAR)

        def drain():
            whole_a().wait_send()
            copy_of(land_x, land_x, sends, recvs, 1, 0).wait_send()
            whole_z().wait_send()

        return start_a, start_b, turn, finish_a, finish_b, drain

    def split_basis():
        def body(rows):
            basis_high[rows, :], basis_low[rows, :] = halves(basis[rows, :])

        blocks(body)
        for i in range(M // 128):
            cols = pl.ds(i * 128, 128)
            turned_high[:, cols], turned_low[:, cols] = halves(jnp.transpose(basis[cols, :]))

    def first_turn():
        def body(rows):
            part_high, part_low = halves(left[rows, :])
            value = dot3(part_high, part_low, basis_high[...], basis_low[...])
            half_high[rows, :], half_low[rows, :] = halves(value)

        blocks(body)

    def second_turn(steps):
        for i in steps:
            rows = pl.ds(i * Q, Q)
            rotated[rows, :] = dot3(turned_high[rows, :], turned_low[rows, :], half_high[...], half_low[...])

            @pl.when(seg < segs - 1)
            def _():
                hand(i).start()

    def hand(i):
        rows = pl.ds(i * Q, Q)
        return pltpu.make_async_remote_copy(
            rotated.at[rows, :], handed_ref.at[rows, :], hand_send.at[i], hand_recv.at[i],
            device_id={"seg": lax.rem(seg + 1, segs)}, device_id_type=MESH,
        )

    def keep(partial, p, value):
        partial[2 * p] = value[:, :HALF].reshape(NX, NZ, ROWS, HALF)
        partial[2 * p + 1] = value[:, HALF:].reshape(NX, NZ, ROWS, HALF)

    def blocks_of(buffer, p):
        return jnp.concatenate([buffer[c].reshape(Q, HALF) for c in (2 * p, 2 * p + 1)], 1)


    def inner(p):
        rows = pl.ds(p * Q, Q)
        value = coefficient * dot3(left_high[:, rows], left_low[:, rows], x_high[rows, :], x_low[rows, :])
        y_high[:, rows], y_low[:, rows] = halves(value)

    def outer(p):
        rows = pl.ds(p * Q, Q)
        return dot3(y_high[rows, :], y_low[rows, :], right_high[:, rows], right_low[:, rows])

    start_a, start_b, pass_a, pass_b, turn, finish, drain_one = gather(gather_one, send_sems[0], recv_sems[0])
    start_b()
    start_a()
    pass_b(0)
    pass_a(0)
    to_left[...] = jnp.where(place == left_place, 1.0, 0.0).astype(BF16)
    loads[3].wait()
    sort_columns(right, to_right, 0)
    sort_columns(right, to_right, 1)
    sort_rows(to_right, scratch_high, right_high)
    turn(ARRIVALS[:2])
    sort_rows(to_right, scratch_low, right_low)
    turn(ARRIVALS[2:])
    loads[4].wait()
    sort_columns(left, to_left, 0)
    sort_columns(left, to_left, 1)
    sort_rows(to_left, scratch_high, left_high)
    sort_rows(to_left, scratch_low, left_low)
    finish()

    loads[6].wait()
    loads[7].wait()
    coefficient = coupling_ref[term_ref[0, 0]]
    masked = jnp.stack([blocks_of(gather_one, p).reshape(OPS, ROWS, Q) for p in range(SECTORS)], 1).reshape(M, Q)
    scale = jnp.sqrt(jnp.sum(masked * masked) / width + 1e-06)
    masked_high, masked_low = halves(masked / scale)
    sorted_high = dot(to_left[...], masked_high)
    sorted_low = dot(to_left[...], masked_low)
    x_high[...] = sorted_high.astype(BF16)
    x_low[...] = sorted_low.astype(BF16)
    initial[...] = sorted_high + sorted_low
    own_initial = own_rows / scale

    for p in range(SECTORS):
        inner(p)
    start_a, start_b, turn, finish_a, finish_b, drain_two = scatter(
        partial_one, land_one, send_sems[1], recv_sems[1]
    )
    for p in range(SECTORS):
        keep(partial_one, p, outer(p))
    start_b()
    start_a()

    loads[5].wait()
    split_basis()
    first_turn()
    turn(Z_GROUPS[:2])
    second_turn((0,))
    turn(Z_GROUPS[2:4])
    second_turn((1,))
    turn(Z_GROUPS[4:])
    gather_a, gather_b, pass_a, pass_b, turn, finish, drain_three = gather(
        gather_two, send_sems[2], recv_sems[2]
    )
    gather_two[0, x, z] = finish_a()
    gather_a()
    pass_a(0)
    gather_two[1:PARTS, x, z] = finish_b()
    gather_b()
    pass_b(0)
    second_turn((2,))

    lane = lax.broadcasted_iota(jnp.int32, (M, 128), 1).astype(F32)
    by_part = position_column[...].reshape(OPS, SECTORS, ROWS, 128)
    by_part = jnp.concatenate([by_part[:, p].reshape(Q, 128) for p in range(SECTORS)], 0)
    for i in range(M // 128):
        hits = by_part == lane + float(i * 128)
        from_left[:, i * 128 : (i + 1) * 128] = jnp.where(hits, 1.0, 0.0).astype(BF16)
    turn(ARRIVALS)
    finish()

    image = jnp.concatenate([blocks_of(gather_two, p) for p in range(SECTORS)], 0)
    start = initial[...]
    energy = jnp.sum(start * image) / width
    spread = jnp.sqrt(jnp.sum(image * image) / width + 1e-06)
    energy_ref[...] = jnp.full((8, 128), energy, F32)
    step = (image - energy * start) / spread
    first[...] = step
    x_high[...], x_low[...] = halves(step)
    for p in range(SECTORS):
        inner(p)
    for p in range(SECTORS):
        out_high, out_low = halves(outer(p))
        rows = pl.ds(p * Q, Q)
        y_high[rows, 0:Q] = out_high
        y_low[rows, 0:Q] = out_low
    start_a, start_b, turn, finish_a, finish_b, drain_four = scatter(
        partial_two, land_two, send_sems[3], recv_sems[3]
    )
    for p in range(SECTORS):
        rows = pl.ds(p * Q, Q)
        back = dot(from_left[rows, :], y_high[:, 0:Q]) + dot(from_left[rows, :], y_low[:, 0:Q])
        keep(partial_two, p, back)
    start_b()
    start_a()

    for drain in (drain_one, drain_two, drain_three):
        drain()
    own_select = jnp.where(
        own_position == lax.broadcasted_iota(jnp.int32, (OWN, M), 1).astype(F32), 1.0, 0.0
    ).astype(BF16)
    own_step = sum(dot(own_select, part) for part in thirds(first[...]))
    turn(Z_GROUPS)
    part, others = finish_a(), finish_b()
    part = [part] + [others[c] for c in range(PARTS - 1)]
    own_image = jnp.concatenate(
        [jnp.concatenate(part[2 * p : 2 * p + 2], 1) for p in range(SECTORS)], 0
    )
    result = 2.0 * (own_image - energy * own_step) / spread - own_initial
    spread_out = jnp.concatenate(
        [
            jnp.where((own_position >= p * Q) & (own_position < (p + 1) * Q), result, 0.0)
            for p in range(SECTORS)
        ],
        1,
    )
    cheb_ref[...] = third_dot(spread_out, to_right[...], NN)

    drain_four()

    @pl.when(seg < segs - 1)
    def _():
        for i in range(SECTORS):
            hand(i).wait_send()

    @pl.when(seg > 0)
    def _():
        for i in range(SECTORS):
            hand(i).wait_recv()

    @pl.when(seg == 0)
    def _():
        kept.wait()


def per_device(
    left_ops,
    right_ops,
    wavefunction,
    basis_rotation,
    pair_term,
    coupling,
    left_charge,
    right_charge,
):
    vmem, hbm = (pl.BlockSpec(memory_space=space) for space in (pltpu.VMEM, pl.ANY))
    dma = pltpu.SemaphoreType.DMA

    def full(dtype):
        return pltpu.VMEM((M, M), dtype)

    def parts():
        return pltpu.VMEM((PARTS, NX, NZ, ROWS, HALF), F32)

    def tall(dtype):
        return pltpu.VMEM((M, Q), dtype)

    land = [
        pltpu.VMEM((OPS, ROWS, HALF), F32), pltpu.VMEM((NZ, NX - 1, PARTS - 1, ROWS, HALF), F32),
        pltpu.VMEM((NZ, PARTS - 1, ROWS, HALF), F32), pltpu.VMEM((NZ, PARTS - 1, ROWS, HALF), F32),
    ]
    cheb, energy, handed = pl.pallas_call(
        kernel,
        name="segment_step",
        out_shape=(pltpu.VMEM((OWN, M), F32), pltpu.VMEM((8, 128), F32), pltpu.VMEM((M, M), F32)),
        in_specs=[hbm] * 8,
        out_specs=(vmem, vmem, vmem),
        scratch_shapes=[
            full(F32), full(F32), full(F32), pltpu.VMEM((OWN, M), F32),
            pltpu.VMEM((1, M), jnp.int32), pltpu.VMEM((1, M), jnp.int32),
            pltpu.SMEM((1, 1), jnp.int32), pltpu.SMEM((16,), F32), dma((9,)),
            full(BF16), full(BF16), full(BF16), full(BF16),
            full(BF16), full(BF16), full(BF16), full(BF16), full(BF16), full(BF16), full(F32),
            full(BF16), full(BF16), full(BF16), pltpu.VMEM((M, 128), F32),
            full(BF16), full(BF16), full(BF16), full(BF16), tall(BF16), tall(BF16),
            tall(F32), tall(F32), parts(), parts(), parts(), parts(),
            list(land), list(land),
            [dma((4,)), dma((3,)), dma((4,)), dma((3,))], [dma((8,)), dma((7,)), dma((8,)), dma((7,))], dma((SECTORS,)), dma((SECTORS,)),
        ],
        compiler_params=pltpu.CompilerParams(
            collective_id=0, has_side_effects=True, vmem_limit_bytes=57 * 2**20
        ),
    )(
        left_ops[0, 0], right_ops[0, 0], basis_rotation[0], wavefunction[0],
        left_charge, right_charge, pair_term, coupling,
    )
    return cheb[None], energy[0, :1], handed[None, None]


def solution(mesh):
    placed = (
        P("seg", "op", None, None),
        P("seg", "op", None, None),
        P("seg", "op", None),
        P("seg", None, None),
        P("seg", "op"),
        P(),
        P("seg", None),
        P("seg", None),
    )
    return jax.shard_map(
        per_device,
        mesh=mesh,
        in_specs=placed,
        out_specs=(P("seg", "op", None), P("seg"), P("seg", "op", None, None)),
        check_vma=False,
    )
```
